256 devices in a mesh: lat: 8 (over y, x_hi), lon: 32 (over x_lo, z, core).
Axes of the slice: x: 4 (x_hi: 2, x_lo: 2; x = x_hi * 2 + x_lo), y: 4, z: 8, core: 2. Of those that a mesh axis runs over, the one named last changes fastest.
Arguments:
- skip: bfloat16 [2, 192, 384, 512], P(None, 'lat', 'lon'), may hold values from -6 to 6
- coarse: bfloat16 [2, 48, 96, 2048], P(None, 'lat', 'lon'), may hold values from -6 to 6
- offsets: int32 [2], replicated, may hold values from 1 to 6, as said below
- bands: int32 [192], replicated, may hold values from 0 to 15, never falling along the last dimension, each value on 1 to 24 neighbouring positions
- qkv3_weight: bfloat16 [2048, 6144], P(None, 'lon')
- out3_weight: bfloat16 [2048, 2048], P('lon'), may hold values from -0.125 to 0.125
- up_weight: bfloat16 [2048, 512], replicated, may hold values from -0.125 to 0.125
- qkv1_weight: bfloat16 [512, 1536], replicated
- out1_weight: bfloat16 [512, 512], replicated, may hold values from -0.25 to 0.25
- mlp_in: bfloat16 [512, 2048], replicated, may hold values from -0.25 to 0.25
- mlp_out: bfloat16 [2048, 512], replicated, may hold values from -0.125 to 0.125
Outputs:
- refined: bfloat16 [2, 192, 384, 512], P(None, 'lat', 'lon')
The draws below stay inside these ranges and needn't reach their ends.
Inputs may be any that keep to these rules, and one draw needn't show every extreme that they name: offsets[0] is the latitude shift and offsets[1] the longitude shift; one of the two equals 6. `bands`: band ids never fall along latitude; one band spans 1 to 24 rows.
All inputs are finite; a program needn't handle non-finite values.
Results may differ from the reference program's by a relative error of at most 0.02.
Values may be sent and summed in bfloat16 or wider, within the bound.
A program may use at most 128 MiB of HBM per device.

```python
import math
import jax
import jax.numpy as jnp
import numpy as np
from jax import lax

D1 = 512
H1 = 8
FF1 = 2048
D3 = 2048
H3 = 32
WLAT = 6
WLON = 12
LEV = 2
SHIFT = 6
LAT = 192
LON = 384


def projection_draw(key, width, heads):
    head_size = width // heads
    base = jax.random.normal(jax.random.fold_in(key, 11), (width, heads, 3, head_size), jnp.float32) * width ** (-0.5)
    keys_part = base[:, :, 1]
    stacked = jnp.stack([base[:, :, 0], keys_part, base[:, :, 2]], axis=2)
    return stacked.reshape(width, 3 * width)


def draw_offsets(key, part):
    key = jax.random.fold_in(key, 1)
    which = jax.random.randint(jax.random.fold_in(key, 2), (), 0, 2)
    other = jax.random.randint(jax.random.fold_in(key, 3), (), 1, SHIFT + 1)
    first = jnp.where(which == 0, SHIFT, other)
    second = jnp.where(which == 0, other, SHIFT)
    return jnp.stack([first, second]).astype(jnp.int32)


def draw_qkv3_weight(key, part):
    key = jax.random.fold_in(key, 3)
    return projection_draw(key, D3, H3).astype(jnp.bfloat16)


def draw_qkv1_weight(key, part):
    key = jax.random.fold_in(key, 5)
    return projection_draw(key, D1, H1).astype(jnp.bfloat16)


def block_scale(key, shape, cuts, smallest, largest):
    loudness = 1.0
    for axis_at, shards_of in cuts:
        heights = jax.random.uniform(jax.random.fold_in(jax.random.fold_in(key, 6), axis_at), (shards_of,), jnp.float32, smallest / len(cuts), largest / len(cuts))
        loudness = loudness * jnp.repeat(jnp.exp(heights), shape[axis_at] // shards_of).reshape((-1,) + (1,) * (len(shape) - 1 - axis_at))
    return loudness


def split_up(number_of, total, most, slope):
    weights = [(1 << 20) // math.isqrt(rank ** slope) + 1 for rank in range(2, number_of + 1)]
    surplus, given = total - most - (number_of - 1), [1] * (number_of - 1)
    while surplus > 0:
        candidates = [i for i in range(number_of - 1) if given[i] < most]
        pool, budget = sum([weights[i] for i in candidates]), surplus
        for i in candidates:
            more = min(most - given[i], max(1, budget * weights[i] // pool), surplus)
            given[i] = given[i] + more
            surplus = surplus - more
    return np.array([most] + given)


def uneven_parts(rng, number_of, total, most, slope):
    if number_of == 2:
        one = jax.random.randint(rng, (), max(1, total - most), min(most, total - 1) + 1)
        return jnp.stack([one, total - one])
    sizes = jnp.asarray(split_up(number_of, total, most, slope), jnp.int32)
    twos = (number_of - 1) // 2
    donor, sink = sizes[1:1 + 2 * twos:2], sizes[2:2 + 2 * twos:2]
    margin = jnp.minimum(donor - 1, most - sink)
    shifted = jax.random.randint(jax.random.fold_in(rng, 1), (twos,), 0, 1 << 20) % (margin + 1)
    sizes = sizes.at[1:1 + 2 * twos:2].set(donor - shifted).at[2:2 + 2 * twos:2].set(sink + shifted)
    return sizes[jax.random.permutation(jax.random.fold_in(rng, 2), number_of)]


def normal_values(rng, dims, scale, reach, pieces=(), dtype=jnp.bfloat16):
    values = scale * jax.random.normal(rng, dims, jnp.float32)
    if pieces:
        values = values * block_scale(rng, dims, pieces, -0.22, 0.18)
    return jnp.clip(values, -reach, reach).astype(dtype)


def setup_inputs(seed: int = 0) -> dict:
    arg_keys = jax.random.split(jax.random.key(seed), 12)
    skip = normal_values(arg_keys[0], (LEV, LAT, LON, D1), 1.0, 6.0, ((1, 8), (2, 32)))
    coarse = normal_values(arg_keys[1], (LEV, LAT // 4, LON // 4, D3), 1.0, 6.0, ((1, 8), (2, 32)))
    offsets = draw_offsets(jax.random.fold_in(arg_keys[11], 71), 0)
    bands = jnp.searchsorted(jnp.cumsum(uneven_parts(arg_keys[3], LAT // 12, LAT, 24, 0)), jnp.arange(LAT), side="right").astype(jnp.int32)
    qkv3_weight = draw_qkv3_weight(jax.random.fold_in(arg_keys[11], 71), 0)
    out3_weight = normal_values(arg_keys[5], (D3, D3), D3 ** -0.5, 0.125, ((0, 32),))
    up_weight = normal_values(arg_keys[6], (D3, D1), D3 ** -0.5, 0.125)
    qkv1_weight = draw_qkv1_weight(jax.random.fold_in(arg_keys[11], 71), 0)
    out1_weight = normal_values(arg_keys[8], (D1, D1), D1 ** -0.5, 0.25)
    mlp_in = normal_values(arg_keys[9], (D1, FF1), D1 ** -0.5, 0.25)
    mlp_out = normal_values(arg_keys[10], (FF1, D1), FF1 ** -0.5, 0.125)
    return {"skip": skip, "coarse": coarse, "offsets": offsets, "bands": bands, "qkv3_weight": qkv3_weight, "out3_weight": out3_weight, "up_weight": up_weight, "qkv1_weight": qkv1_weight, "out1_weight": out1_weight, "mlp_in": mlp_in, "mlp_out": mlp_out}


EPS = 1e-05

def normalize(values):
    centred = values - lax.optimization_barrier(jnp.mean(values, axis=-1, keepdims=True))
    spread = lax.optimization_barrier(jnp.mean(centred * centred, axis=-1, keepdims=True))
    return centred * lax.rsqrt(spread + EPS)

def attend(packed, allowed):
    queries = packed[..., 0, :].astype(jnp.float32)
    keys = packed[..., 1, :].astype(jnp.float32)
    values = packed[..., 2, :].astype(jnp.float32)
    scale = packed.shape[-1] ** (-0.5)
    scores = jnp.einsum('lxiyjhd,mxkynhd->xyhlijmkn', queries, keys) * scale
    scores = jnp.where(allowed[:, None, None, None, :, None, None, :, None], scores, -jnp.inf)
    highest = lax.optimization_barrier(jnp.max(scores, axis=(6, 7, 8), keepdims=True))
    weights = jnp.exp(scores - highest)
    probs = (weights / lax.optimization_barrier(jnp.sum(weights, axis=(6, 7, 8), keepdims=True))).astype(jnp.bfloat16)
    mixed = jnp.einsum('xyhlijmkn,mxkynhd->lxiyjhd', probs.astype(jnp.float32), values)
    return mixed.astype(jnp.bfloat16)

def windows_by_row(packed, allowed):
    moved = jnp.moveaxis(packed, 1, 0)

    def one_row(pair):
        block, mask = pair
        return attend(block[:, None], mask[None])[:, 0]
    mixed = lax.map(one_row, (moved, allowed))
    return jnp.moveaxis(mixed, 0, 1)

def by_blocks(function, rows, count):
    total = rows.shape[0]
    shaped = rows.reshape(count, total // count, rows.shape[1])
    result = lax.map(function, shaped)
    return result.reshape(total, result.shape[-1])

def reference(skip, coarse, offsets, bands, qkv3_weight, out3_weight, up_weight, qkv1_weight, out1_weight, mlp_in, mlp_out):
    levels, coarse_lat, coarse_lon, width_coarse = coarse.shape
    head_coarse = width_coarse // H3
    normed3 = normalize(coarse.astype(jnp.float32)).astype(jnp.bfloat16).reshape(-1, width_coarse)
    packed3 = jnp.dot(normed3, qkv3_weight, preferred_element_type=jnp.float32).astype(jnp.bfloat16)
    packed3 = packed3.reshape(levels, coarse_lat // WLAT, WLAT, coarse_lon // WLON, WLON, H3, 3, head_coarse)
    open_mask = jnp.zeros((coarse_lat // WLAT, WLAT, WLAT), jnp.int32) == 0
    mixed3 = windows_by_row(packed3, open_mask).reshape(-1, width_coarse)
    summed = jnp.dot(mixed3, out3_weight, preferred_element_type=jnp.float32)
    updated = coarse.reshape(-1, width_coarse).astype(jnp.float32) + summed
    lifted = jnp.dot(updated, up_weight.astype(jnp.float32), precision=lax.Precision.HIGHEST, preferred_element_type=jnp.float32)
    width_fine = skip.shape[-1]
    lifted = lifted.reshape(levels, coarse_lat, coarse_lon, width_fine)
    expanded = jnp.repeat(jnp.repeat(lifted, 4, axis=1), 4, axis=2)
    stream = skip.astype(jnp.float32) + expanded
    fine_lat, fine_lon = (skip.shape[1], skip.shape[2])
    head_fine = width_fine // H1

    def project_block(block):
        normed = normalize(block).astype(jnp.bfloat16)
        return jnp.dot(normed, qkv1_weight, preferred_element_type=jnp.float32).astype(jnp.bfloat16)
    packed1 = by_blocks(project_block, stream.reshape(-1, width_fine), 64)
    packed1 = packed1.reshape(levels, fine_lat, fine_lon, 3 * width_fine)
    lat_shift = offsets[0]
    lon_shift = offsets[1]
    rolled = jnp.roll(jnp.roll(packed1, -lat_shift, axis=1), -lon_shift, axis=2)
    labels = jnp.roll(bands, -lat_shift).reshape(fine_lat // WLAT, WLAT)
    allowed = labels[:, :, None] == labels[:, None, :]
    rolled = rolled.reshape(levels, fine_lat // WLAT, WLAT, fine_lon // WLON, WLON, H1, 3, head_fine)
    mixed1 = windows_by_row(rolled, allowed).reshape(levels, fine_lat, fine_lon, width_fine)
    mixed1 = jnp.roll(jnp.roll(mixed1, lat_shift, axis=1), lon_shift, axis=2)
    joined = jnp.concatenate([stream.reshape(-1, width_fine), mixed1.reshape(-1, width_fine).astype(jnp.float32)], axis=1)

    def finish_block(block):
        residual = block[:, :width_fine]
        mixed_rows = block[:, width_fine:].astype(jnp.bfloat16)
        attended = residual + jnp.dot(mixed_rows, out1_weight, preferred_element_type=jnp.float32)
        normed2 = normalize(attended).astype(jnp.bfloat16)
        hidden = jax.nn.gelu(jnp.dot(normed2, mlp_in, preferred_element_type=jnp.float32)).astype(jnp.bfloat16)
        return (attended + jnp.dot(hidden, mlp_out, preferred_element_type=jnp.float32)).astype(jnp.bfloat16)
    refined = by_blocks(finish_block, joined, 64)
    return refined.reshape(levels, fine_lat, fine_lon, width_fine)
```

```python
import jax
import jax.numpy as jnp
from jax import lax
from jax.experimental import pallas as pl
from jax.experimental.pallas import tpu as pltpu
from jax.sharding import PartitionSpec as P

LATS = 8
LONS = 32
ROWS = 192
D3 = 2048
D1 = 512
FF = 2048
HEAD = 64
CELLS3 = 36
SCALE = HEAD**-0.5
EPS = 1e-05
HALF = 80
WIN = 2 * HALF
MASKED = -1e30

F32 = jnp.float32
BF = jnp.bfloat16
MESH = pl.DeviceIdType.MESH
ANY = pl.ANY


def dot(a, b):
    return jnp.dot(a, b, preferred_element_type=F32)


def dot_nt(a, b):
    return lax.dot_general(a, b, (((1,), (1,)), ((), ())), preferred_element_type=F32)


def normalize(values):
    centred = values - jnp.mean(values, axis=-1, keepdims=True)
    spread = jnp.mean(centred * centred, axis=-1, keepdims=True)
    return centred * lax.rsqrt(spread + EPS)


def column(n):
    return lax.broadcasted_iota(jnp.int32, (n, 1), 0)


def onehot(target, width):
    n = target.shape[0]
    hit = lax.broadcasted_iota(jnp.int32, (n, width), 1) == target
    return jnp.where(hit, 1.0, 0.0).astype(BF)


def frame_cell(n):
    half = (n >= HALF).astype(jnp.int32)
    m = n - HALF * half
    valid = m < 72
    level = (m >= 36).astype(jnp.int32)
    m = m - 36 * level
    row = (m * 43) >> 8
    return valid, level, row, m - 6 * row + 6 * half


def softmax_mix(q, k, v, bias):
    scores = dot_nt(q, k) * SCALE
    if bias is not None:
        scores = scores + bias
    weights = jnp.exp(scores - jnp.max(scores, axis=1, keepdims=True))
    total = jnp.sum(weights, axis=1, keepdims=True)
    return dot(weights.astype(BF), v) * (1.0 / total)


def kernel(
    offs,
    bands,
    coarse,
    skip,
    wq,
    wo,
    up,
    w1,
    wo1,
    wi,
    wf,
    out,
    xs,
    G,
    Wb,
    wov,
    upv,
    W4,
    cup,
    skv,
    Sp,
    E,
    skF,
    bias,
    Pl,
    Po,
    Xt,
    PK,
    msg,
    R,
    LE,
    w1v,
    wo1v,
    wiv,
    wfv,
    pk1,
    mix,
    Z,
    loc,
    own_send,
    ring_send,
    ring_recv,
    wx_send,
    wx_recv,
    ws_send,
    ws_recv,
    wr_send,
    wr_recv,
    w4_send,
    w4_recv,
    sk_send,
    sk_recv,
    aa_send,
    aa_recv,
    li_send,
    li_recv,
    lo_send,
    lo_recv,
    la_send,
    la_recv,
):
    lat = lax.axis_index("lat")
    lon = lax.axis_index("lon")
    xl = lon // 16
    z = lax.rem(lon // 2, 8)
    c = lax.rem(lon, 2)
    base = xl * 16

    def at(lat_, lon_):
        return {"lat": lat_, "lon": lon_}

    def chip(z_, c_):
        return at(lat, base + 2 * lax.rem(z_ + 8, 8) + c_)

    sibling = at(lat, lon + 1 - 2 * c)
    across = lax.rem(lon + 16, 32)
    near = at(lat, across)
    far = at(lat + 1 - 2 * lax.rem(lat, 2), across)
    lon_next = lax.rem(lon + 1, LONS)
    lon_prev = lax.rem(lon + LONS - 1, LONS)
    lat_next = lax.rem(lat + 1, LATS)
    lat_prev = lax.rem(lat + LATS - 1, LATS)

    def remote(src, dst, send, recv, device):
        return pltpu.make_async_remote_copy(
            src_ref=src, dst_ref=dst, send_sem=send, recv_sem=recv, device_id=device, device_id_type=MESH
        )

    loads = [
        pltpu.make_async_copy(src, dst, loc.at[i])
        for i, (src, dst) in enumerate(
            [(up, upv), (wo, wov), (wq, Wb.at[0]), (skip, skv), (w1, w1v), (wo1, wo1v), (wi, wiv), (wf, wfv)]
        )
    ]
    for load in loads:
        load.start()

    barrier = pltpu.get_barrier_semaphore()
    greeted = [chip(z + d, c_) for d in range(1, 8) for c_ in (0, 1)] + [
        sibling,
        near,
        far,
        at(lat, lon_next),
        at(lat, lon_prev),
        at(lat_next, lon),
        at(lat_prev, lon),
        at(lat_next, lon_next),
        at(lat_prev, lon_prev),
    ]
    for device in greeted:
        pl.semaphore_signal(barrier, inc=1, device_id=device, device_id_type=MESH)

    normed3 = normalize(coarse[...].astype(F32)).astype(BF)
    rest = jnp.zeros((16, 512), F32)
    i16 = column(16)
    for f in range(4):
        part = normed3[:, 512 * f : 512 * f + 512]
        xs[32 * f : 32 * f + 32, :] = part[0:32]
        pick = onehot(jnp.where((i16 >> 2) == f, i16 & 3, -1), 16)
        rest = rest + dot(pick, part[32:48])
    xs[128:144, :] = rest.astype(BF)

    pl.semaphore_wait(barrier, len(greeted))

    target = z // 4
    mine = lax.rem(z, 4) * 2 + c
    is_home = target == c
    own = [
        remote(xs, G.at[mine], own_send.at[0], ring_recv.at[mine], chip(z + 1, target)),
        remote(xs, G.at[mine], own_send.at[1], ring_recv.at[mine], chip(z - 1, target)),
    ]
    own_sib = remote(xs, G.at[mine], own_send.at[2], ring_recv.at[mine], sibling)
    for copy in own:
        copy.start()

    @pl.when(jnp.logical_not(is_home))
    def _():
        own_sib.start()

    def rows(j):
        return pl.ds(512 * j, 512)

    wx = [
        remote(wq.at[rows(j)], Wb.at[2, rows(j)], wx_send.at[j], wx_recv.at[j], near if j < 2 else far)
        for j in (0, 2, 1, 3)
    ]
    for copy in wx:
        copy.start()
    ws = remote(wq, Wb.at[1], ws_send.at[0], ws_recv.at[0], sibling)
    ws.start()

    loads[0].wait()
    loads[1].wait()
    W4[0:64, :] = dot(wov[...], upv[...]).astype(BF)
    w4x = remote(W4.at[0:64], W4.at[128:192], w4_send.at[0], w4_recv.at[0], near)
    w4x.start()
    w4s = remote(W4.at[0:64], W4.at[64:128], w4_send.at[1], w4_recv.at[1], sibling)
    w4s.start()
    cup[...] = dot(coarse[...], upv[...])

    @pl.when(is_home)
    def _():
        G[pl.ds(mine, 1)] = xs[...].reshape(1, 144, 512)

    def relay(k, way):
        return remote(
            G.at[k], G.at[k], ring_send.at[k, way], ring_recv.at[k], chip(z + (1 if way == 0 else -1), c)
        )

    def ring_steps(s):
        for way in (0, 1):
            source = lax.rem(z + (8 - s if way == 0 else s), 8)
            for core in (0, 1):
                limit = 4 if core == way else 3
                if s <= limit:
                    yield way, lax.rem(source, 4) * 2 + core, source // 4 == c, s < limit

    def ring(s):
        for way, k, here, onward in ring_steps(s):

            @pl.when(here)
            def _(way=way, k=k, onward=onward):
                copy = relay(k, way)
                copy.wait_recv()
                if onward:
                    copy.start()

    ring(1)

    loads[3].wait()
    Sp[...] = jnp.zeros_like(Sp)
    for k in range(48):
        Sp[16 * k : 16 * k + 12, :] = skv[k]
    r192 = column(192)
    spread = onehot(((r192 >> 3) & 1) * 128 + (r192 & 7) * 16 + (r192 >> 4), 256)
    for b in range(3):
        E[b, 0:192, :] = (
            dot(spread[:, 0:128], Sp[128 * b : 128 * b + 128, :])
            + dot(spread[:, 128:256], Sp[384 + 128 * b : 384 + 128 * b + 128, :])
        ).astype(BF)

    ring(2)

    a = offs[0]
    shift_lat = jnp.where(a >= 6, a - 6, a)
    shift_lon = offs[1]
    n = column(WIN)
    valid, level, row, col = frame_cell(n)
    valid_t, _, row_t, _ = frame_cell(lax.broadcasted_iota(jnp.int32, (1, WIN), 1))
    source_col = col + shift_lon
    for w in range(4):
        source_row = row + (shift_lat + 6 * w)
        over = (source_row >= 24).astype(jnp.int32)
        coarse_row = source_row >> 2
        coarse_col = source_col >> 2
        row_out = (coarse_row >= 6).astype(jnp.int32)
        col_out = (coarse_col >= 3).astype(jnp.int32)
        cell = 48 * (col_out + 2 * row_out) + 18 * level + 3 * (coarse_row - 6 * row_out) + coarse_col - 3 * col_out
        Pl[w] = onehot(jnp.where(valid, cell, -1), 192)
        label = jnp.zeros((WIN, 1), jnp.int32)
        label_t = jnp.zeros((1, WIN), jnp.int32)
        for i in range(6):
            band = bands[lax.rem(lat * 24 + shift_lat + (6 * w + i), ROWS)]
            label = jnp.where(row == i, band, label)
            label_t = jnp.where(row_t == i, band, label_t)
        free = jnp.where(valid, 0, 1)
        seen = jnp.where(valid_t, 1, 0)
        match = jnp.where(label == label_t, 1, 0)
        bias[w] = jnp.where(seen * (match + free) > 0, 0.0, MASKED)

    r = column(192)
    out_level = (r >= 96).astype(jnp.int32)
    out_col = r & 15
    frame_row = ((r - 96 * out_level) >> 4) - shift_lat
    before = (frame_row < 0).astype(jnp.int32)
    inner = 36 * out_level + 6 * (frame_row + 6 * before)
    frame_col = out_col - shift_lon
    left = frame_col < 0
    second = (frame_col >= 6).astype(jnp.int32)
    place = jnp.where(left, 160 + 6 + frame_col, HALF * second + frame_col - 6 * second)
    Po[...] = onehot(jnp.where(out_col < 12, 240 * (1 - before) + inner + place, -1), 480)

    ring(3)

    sk = [
        remote(E.at[0:3, 0:96], E.at[0:3, 192:288], sk_send.at[0], sk_recv.at[0], at(lat, lon_prev)),
        remote(E.at[0, 0:192], E.at[3, 0:192], sk_send.at[1], sk_recv.at[1], at(lat_prev, lon)),
        remote(E.at[0, 0:96], E.at[3, 192:288], sk_send.at[2], sk_recv.at[2], at(lat_prev, lon_prev)),
    ]
    for copy in sk:
        copy.start()

    w4x.wait_recv()
    w4r = remote(W4.at[128:192], W4.at[192:256], w4_send.at[2], w4_recv.at[2], sibling)
    w4r.start()
    wr = [
        remote(Wb.at[2, rows(j)], Wb.at[3, rows(j)], wr_send.at[j], wr_recv.at[j], sibling) for j in (0, 2, 1, 3)
    ]
    for arrived, onward in zip(wx, wr):
        arrived.wait_recv()
        onward.start()

    ring(4)

    @pl.when(is_home)
    def _():
        k = lax.rem(z, 4) * 2 + (1 - c)
        remote(xs, G.at[k], own_send.at[2], ring_recv.at[k], sibling).wait_recv()

    for w in range(2):
        tails = G[4 * w : 4 * w + 4, 128:144, :].reshape(64, 512)
        for f in range(4):
            pick = onehot((i16 >> 2) * 16 + 4 * f + (i16 & 3), 64)
            Xt[16 * w : 16 * w + 16, 512 * f : 512 * f + 512] = dot(pick, tails).astype(BF)

    loads[2].wait()
    ws.wait_recv()
    for copy in wr:
        copy.wait_recv()
    w4s.wait_recv()
    w4r.wait_recv()

    for h in range(4):
        main = jnp.zeros((256, 192), F32)
        for f in range(4):
            main = main + dot(
                G[:, 32 * f : 32 * f + 32, :].reshape(256, 512), Wb[h, 512 * f : 512 * f + 512, :]
            )
        tail = dot(Xt[...], Wb[h])
        for w in range(2):
            PK[h, w, 0:128, :] = main[128 * w : 128 * w + 128].astype(BF)
            PK[h, w, 128:144, :] = tail[16 * w : 16 * w + 16].astype(BF)

    i64 = column(64)
    for w in range(2):
        terms = jnp.zeros((144, 512), F32)
        for h in range(4):
            packed = PK[h, w]
            mixed = softmax_mix(packed[:, 0:64], packed[:, 64:128], packed[:, 128:192], None).astype(BF)
            terms = terms + dot(mixed, W4[64 * h : 64 * h + 64, :])
        terms = terms.astype(BF)
        tails = jnp.zeros((64, 128), F32)
        for f in range(4):
            part = terms[:, 128 * f : 128 * f + 128]
            for q in range(4):
                msg[4 * w + q, 32 * f : 32 * f + 32, :] = part[32 * q : 32 * q + 32]
            tails = tails + dot(
                onehot(jnp.where(((i64 >> 2) & 3) == f, (i64 >> 4) * 4 + (i64 & 3), -1), 16), part[128:144]
            )
        tails = tails.astype(BF)
        for q in range(4):
            msg[4 * w + q, 128:144, :] = tails[16 * q : 16 * q + 16]

    def term(k):
        return remote(msg.at[k], R.at[z], aa_send.at[k], aa_recv.at[z], at(lat, base + 8 * c + k))

    for k in range(8):

        @pl.when(base + 8 * c + k != lon)
        def _(k=k):
            term(k).start()

    @pl.when(is_home)
    def _():
        R[pl.ds(z, 1)] = msg[pl.ds(mine, 1)]

    total = jnp.zeros((144, 128), F32)
    for s in range(8):

        @pl.when(base + 2 * s + target != lon)
        def _(s=s):
            remote(msg.at[0], R.at[s], aa_send.at[0], aa_recv.at[s], sibling).wait_recv()

    for s in range(8):
        total = total + R[s].astype(F32)
    for f in range(4):
        lanes = slice(128 * f, 128 * f + 128)
        LE[0:32, lanes] = (cup[0:32, lanes] + total[32 * f : 32 * f + 32]).astype(BF)
        pick = jnp.where(
            (lax.broadcasted_iota(jnp.int32, (16, 16), 1) == 4 * f + i16) & (i16 < 4), 1.0, 0.0
        )
        rest = jnp.dot(pick, total[128:144], preferred_element_type=F32, precision=lax.Precision.HIGHEST)
        LE[32:48, lanes] = (cup[32:48, lanes] + rest).astype(BF)

    li = [
        remote(LE.at[0:48], LE.at[48:96], li_send.at[0], li_recv.at[0], at(lat, lon_prev)),
        remote(LE.at[0:48], LE.at[96:144], li_send.at[1], li_recv.at[1], at(lat_prev, lon)),
        remote(LE.at[0:48], LE.at[144:192], li_send.at[2], li_recv.at[2], at(lat_prev, lon_prev)),
    ]
    for copy in li:
        copy.start()

    for copy in sk:
        copy.wait_recv()
    for w in range(4):
        source_row = row + (shift_lat + 6 * w)
        first = w // 2
        cell = 288 * ((source_row >> 3) - first) + 16 * source_col + 8 * level + (source_row & 7)
        cell = jnp.where(valid, cell, -1)
        taken = jnp.zeros((WIN, D1), F32)
        for b in range(3):
            taken = taken + dot(onehot(cell - 288 * b, 288), E[first + b])
        skF[w] = taken.astype(BF)

    for load in loads[4:]:
        load.wait()
    for copy in li:
        copy.wait_recv()

    def window(t, carry):
        w = lax.rem(t + 3, 4)
        stream = skF[w].astype(F32) + dot(Pl[w], LE[...])
        pk1[...] = dot(normalize(stream).astype(BF), w1v[...]).astype(BF)
        allowed = bias[w]
        for pair in range(4):
            both = []
            for h in (2 * pair, 2 * pair + 1):
                q = pk1[:, 192 * h : 192 * h + 64]
                k = pk1[:, 192 * h + 64 : 192 * h + 128]
                v = pk1[:, 192 * h + 128 : 192 * h + 192]
                both.append(softmax_mix(q, k, v, allowed))
            mix[:, 128 * pair : 128 * pair + 128] = jnp.concatenate(both, axis=1).astype(BF)
        attended = stream + dot(mix[...], wo1v[...])
        normed2 = normalize(attended).astype(BF)
        result = attended
        for f in range(2):
            hidden = jax.nn.gelu(dot(normed2, wiv[:, 1024 * f : 1024 * f + 1024])).astype(BF)
            result = result + dot(hidden, wfv[1024 * f : 1024 * f + 1024, :])
        Z[w + 1, 0:WIN, :] = result.astype(BF)
        to_lon(w).start()

        @pl.when(t == 0)
        def _():
            to_lat.start()
            to_both.start()

        return carry

    def to_lon(w):
        return remote(
            Z.at[w + 1, HALF:WIN], Z.at[w + 1, WIN : WIN + HALF], lo_send.at[w], lo_recv.at[w], at(lat, lon_next)
        )

    to_lat = remote(Z.at[4, 0:WIN], Z.at[0, 0:WIN], la_send.at[0], la_recv.at[0], at(lat_next, lon))
    to_both = remote(
        Z.at[4, HALF:WIN], Z.at[0, WIN : WIN + HALF], la_send.at[1], la_recv.at[1], at(lat_next, lon_next)
    )
    lax.fori_loop(0, 4, window, 0)

    to_lat.wait_recv()
    to_both.wait_recv()
    for w in (3, 0, 1, 2):
        to_lon(w).wait_recv()
    for v in range(4):
        taken = dot(Po[:, 0:240], Z[v]) + dot(Po[:, 240:480], Z[v + 1])
        taken = taken.astype(BF)
        out[96 * v : 96 * v + 96, :] = taken[0:96]
        out[384 + 96 * v : 384 + 96 * v + 96, :] = taken[96:192]

    for copy in [*own, *wx, ws, w4x, w4s, w4r, *wr, *sk, *li, to_lat, to_both]:
        copy.wait_send()

    @pl.when(jnp.logical_not(is_home))
    def _():
        own_sib.wait_send()

    for s in (1, 2, 3):
        for way, k, here, onward in ring_steps(s):
            if onward:

                @pl.when(here)
                def _(way=way, k=k):
                    relay(k, way).wait_send()

    for k in range(8):

        @pl.when(base + 8 * c + k != lon)
        def _(k=k):
            term(k).wait_send()

    for w in range(4):
        to_lon(w).wait_send()


def local(
    skip,
    coarse,
    offsets,
    bands,
    qkv3_weight,
    out3_weight,
    up_weight,
    qkv1_weight,
    out1_weight,
    mlp_in,
    mlp_out,
):
    cells = jnp.pad(coarse.reshape(CELLS3, D3), ((0, 12), (0, 0)))
    vmem = pl.BlockSpec(memory_space=pltpu.VMEM)
    smem = pl.BlockSpec(memory_space=pltpu.SMEM)
    hbm = pl.BlockSpec(memory_space=ANY)
    dma = pltpu.SemaphoreType.DMA
    placed = pl.pallas_call(
        kernel,
        out_shape=jax.ShapeDtypeStruct((768, D1), BF),
        in_specs=[smem, smem, vmem] + [hbm] * 8,
        out_specs=vmem,
        scratch_shapes=[
            pltpu.VMEM((144, 512), BF),
            pltpu.VMEM((8, 144, 512), BF),
            pltpu.VMEM((4, D3, 192), BF),
            pltpu.VMEM((64, D3), BF),
            pltpu.VMEM((D3, D1), BF),
            pltpu.VMEM((256, D1), BF),
            pltpu.VMEM((48, D1), F32),
            pltpu.VMEM((48, 12, D1), BF),
            pltpu.VMEM((768, D1), BF),
            pltpu.VMEM((4, 288, D1), BF),
            pltpu.VMEM((4, WIN, D1), BF),
            pltpu.VMEM((4, WIN, WIN), F32),
            pltpu.VMEM((4, WIN, 192), BF),
            pltpu.VMEM((192, 480), BF),
            pltpu.VMEM((32, D3), BF),
            pltpu.VMEM((4, 2, 144, 192), BF),
            pltpu.VMEM((8, 144, 128), BF),
            pltpu.VMEM((8, 144, 128), BF),
            pltpu.VMEM((192, D1), BF),
            pltpu.VMEM((D1, 3 * D1), BF),
            pltpu.VMEM((D1, D1), BF),
            pltpu.VMEM((D1, FF), BF),
            pltpu.VMEM((FF, D1), BF),
            pltpu.VMEM((WIN, 3 * D1), BF),
            pltpu.VMEM((WIN, D1), BF),
            pltpu.VMEM((5, 240, D1), BF),
            dma((8,)),
            dma((3,)),
            dma((8, 2)),
            dma((8,)),
            dma((4,)),
            dma((4,)),
            dma((1,)),
            dma((1,)),
            dma((4,)),
            dma((4,)),
            dma((3,)),
            dma((3,)),
            dma((3,)),
            dma((3,)),
            dma((8,)),
            dma((8,)),
            dma((3,)),
            dma((3,)),
            dma((4,)),
            dma((4,)),
            dma((2,)),
            dma((2,)),
        ],
        compiler_params=pltpu.CompilerParams(
            collective_id=0, has_side_effects=True, vmem_limit_bytes=56 * 1024 * 1024
        ),
    )(
        offsets,
        bands,
        cells,
        skip.reshape(48, 12, D1),
        qkv3_weight,
        out3_weight,
        up_weight,
        qkv1_weight,
        out1_weight,
        mlp_in,
        mlp_out,
    )
    return placed.reshape(2, 24, 16, D1)[:, :, :12]


def solution(mesh):
    return jax.shard_map(
        local,
        mesh=mesh,
        in_specs=(
            P(None, "lat", "lon", None),
            P(None, "lat", "lon", None),
            P(),
            P(),
            P(None, "lon"),
            P("lon", None),
            P(),
            P(),
            P(),
            P(),
            P(),
        ),
        out_specs=P(None, "lat", "lon", None),
        check_vma=False,
    )
```

```python
import jax
import jax.numpy as jnp
from jax import lax
from jax.experimental import pallas as pl
from jax.experimental.pallas import tpu as pltpu
from jax.sharding import PartitionSpec as P

LATS = 8
LONS = 32
ROWS = 192
D3 = 2048
D1 = 512
FF = 2048
HEAD = 64
CELLS3 = 36
OWN = 576
SCALE = HEAD**-0.5
EPS = 1e-05
HALF = 80
WIN = 2 * HALF
MASKED = -1e30

F32 = jnp.float32
BF = jnp.bfloat16
MESH = pl.DeviceIdType.MESH
ANY = pl.ANY


def dot(a, b):
    return jnp.dot(a, b, preferred_element_type=F32)


def dot_nt(a, b):
    return lax.dot_general(a, b, (((1,), (1,)), ((), ())), preferred_element_type=F32)


def normalize(values):
    centred = values - jnp.mean(values, axis=-1, keepdims=True)
    spread = jnp.mean(centred * centred, axis=-1, keepdims=True)
    return centred * lax.rsqrt(spread + EPS)


def column(n):
    return lax.broadcasted_iota(jnp.int32, (n, 1), 0)


def onehot(target, width):
    n = target.shape[0]
    hit = lax.broadcasted_iota(jnp.int32, (n, width), 1) == target
    return jnp.where(hit, 1.0, 0.0).astype(BF)


def frame_cell(n):
    half = (n >= HALF).astype(jnp.int32)
    m = n - HALF * half
    valid = m < 72
    level = (m >= 36).astype(jnp.int32)
    m = m - 36 * level
    row = (m * 43) >> 8
    return valid, level, row, m - 6 * row + 6 * half


def softmax_mix(q, k, v, bias):
    scores = dot_nt(q, k) * SCALE
    if bias is not None:
        scores = scores + bias
    weights = jnp.exp(scores - jnp.max(scores, axis=1, keepdims=True))
    total = jnp.sum(weights, axis=1, keepdims=True)
    return dot(weights.astype(BF), v) * (1.0 / total)


def kernel(
    offs,
    bands,
    coarse,
    skip,
    wq,
    wo,
    up,
    w1,
    wo1,
    wi,
    wf,
    out,
    xs,
    G,
    Wb,
    wov,
    upv,
    W4,
    cup,
    Sp,
    E,
    skF,
    bias,
    Pl,
    Po,
    Xt,
    PK,
    msg,
    R,
    LE,
    w1v,
    wo1v,
    wiv,
    wfv,
    pk1,
    mix,
    Z,
    loc,
    own_send,
    ring_send,
    ring_recv,
    wx_send,
    wx_recv,
    ws_send,
    ws_recv,
    wr_send,
    wr_recv,
    w4_send,
    w4_recv,
    sk_send,
    sk_recv,
    aa_send,
    aa_recv,
    li_send,
    li_recv,
    lo_send,
    lo_recv,
    la_send,
    la_recv,
):
    lat = lax.axis_index("lat")
    lon = lax.axis_index("lon")
    xl = lon // 16
    z = lax.rem(lon // 2, 8)
    c = lax.rem(lon, 2)
    base = xl * 16

    def at(lat_, lon_):
        return {"lat": lat_, "lon": lon_}

    def chip(z_, c_):
        return at(lat, base + 2 * lax.rem(z_ + 8, 8) + c_)

    sibling = at(lat, lon + 1 - 2 * c)
    across = lax.rem(lon + 16, 32)
    near = at(lat, across)
    far = at(lat + 1 - 2 * lax.rem(lat, 2), across)
    lon_next = lax.rem(lon + 1, LONS)
    lon_prev = lax.rem(lon + LONS - 1, LONS)
    lat_next = lax.rem(lat + 1, LATS)
    lat_prev = lax.rem(lat + LATS - 1, LATS)

    def remote(src, dst, send, recv, device):
        return pltpu.make_async_remote_copy(
            src_ref=src, dst_ref=dst, send_sem=send, recv_sem=recv, device_id=device, device_id_type=MESH
        )

    loads = [
        pltpu.make_async_copy(src, dst, loc.at[i])
        for i, (src, dst) in enumerate(
            [(up, upv), (wo, wov), (wq, Wb.at[0]), (skip, E.at[0:OWN]), (w1, w1v), (wo1, wo1v), (wi, wiv), (wf, wfv)]
        )
    ]
    for load in loads:
        load.start()

    barrier = pltpu.get_barrier_semaphore()
    greeted = [chip(z + d, c_) for d in range(1, 8) for c_ in (0, 1)] + [
        sibling,
        near,
        far,
        at(lat, lon_next),
        at(lat, lon_prev),
        at(lat_next, lon),
        at(lat_prev, lon),
        at(lat_next, lon_next),
        at(lat_prev, lon_prev),
    ]
    for device in greeted:
        pl.semaphore_signal(barrier, inc=1, device_id=device, device_id_type=MESH)

    cells = coarse[...].astype(F32).reshape(CELLS3, D3)
    cells = jnp.concatenate([cells, jnp.zeros((12, D3), F32)], axis=0)
    normed3 = normalize(cells).astype(BF)
    cells = cells.astype(BF)
    rest = jnp.zeros((16, 512), F32)
    i16 = column(16)
    for f in range(4):
        part = normed3[:, 512 * f : 512 * f + 512]
        xs[32 * f : 32 * f + 32, :] = part[0:32]
        pick = onehot(jnp.where((i16 >> 2) == f, i16 & 3, -1), 16)
        rest = rest + dot(pick, part[32:48])
    xs[128:144, :] = rest.astype(BF)

    pl.semaphore_wait(barrier, len(greeted))

    target = z // 4
    mine = lax.rem(z, 4) * 2 + c
    is_home = target == c
    own = [
        remote(xs, G.at[mine], own_send.at[0], ring_recv.at[mine], chip(z + 1, target)),
        remote(xs, G.at[mine], own_send.at[1], ring_recv.at[mine], chip(z - 1, target)),
    ]
    own_sib = remote(xs, G.at[mine], own_send.at[2], ring_recv.at[mine], sibling)
    for copy in own:
        copy.start()

    @pl.when(jnp.logical_not(is_home))
    def _():
        own_sib.start()

    def rows(j):
        return pl.ds(48 * j, 48)

    wx = [
        remote(wq.at[rows(j)], Wb.at[2, rows(j)], wx_send.at[j], wx_recv.at[j], near if j < 2 else far)
        for j in (0, 2, 1, 3)
    ]
    for copy in wx:
        copy.start()
    ws = remote(wq, Wb.at[1], ws_send.at[0], ws_recv.at[0], sibling)
    ws.start()

    loads[0].wait()
    loads[1].wait()
    W4[0:64, :] = dot(wov[...], upv[...]).astype(BF)
    w4x = remote(W4.at[0:64], W4.at[128:192], w4_send.at[0], w4_recv.at[0], near)
    w4x.start()
    w4s = remote(W4.at[0:64], W4.at[64:128], w4_send.at[1], w4_recv.at[1], sibling)
    w4s.start()
    cup[...] = dot(cells, upv[...])

    @pl.when(is_home)
    def _():
        G[pl.ds(mine, 1)] = xs[...].reshape(1, 144, 512)

    def relay(k, way):
        return remote(
            G.at[k], G.at[k], ring_send.at[k, way], ring_recv.at[k], chip(z + (1 if way == 0 else -1), c)
        )

    def ring_steps(s):
        for way in (0, 1):
            source = lax.rem(z + (8 - s if way == 0 else s), 8)
            for core in (0, 1):
                limit = 4 if core == way else 3
                if s <= limit:
                    yield way, lax.rem(source, 4) * 2 + core, source // 4 == c, s < limit

    def ring(s):
        for way, k, here, onward in ring_steps(s):

            @pl.when(here)
            def _(way=way, k=k, onward=onward):
                copy = relay(k, way)
                copy.wait_recv()
                if onward:
                    copy.start()

    ring(1)

    loads[3].wait()
    r192 = column(192)
    first_rows = onehot(((r192 >> 3) & 1) * 288 + (r192 >> 4) * 24 + (r192 & 7), OWN)
    Sp[...] = dot(first_rows, E[0:OWN, :]).astype(BF)

    ring(2)

    a = offs[0]
    shift_lat = jnp.where(a >= 6, a - 6, a)
    shift_lon = offs[1]
    n = column(WIN)
    valid, level, row, col = frame_cell(n)
    valid_t, _, row_t, _ = frame_cell(lax.broadcasted_iota(jnp.int32, (1, WIN), 1))
    source_col = col + shift_lon
    for w in range(4):
        source_row = row + (shift_lat + 6 * w)
        coarse_row = source_row >> 2
        coarse_col = source_col >> 2
        row_out = (coarse_row >= 6).astype(jnp.int32)
        col_out = (coarse_col >= 3).astype(jnp.int32)
        cell = 48 * (col_out + 2 * row_out) + level + 6 * (coarse_row - 6 * row_out) + 2 * (coarse_col - 3 * col_out)
        Pl[w] = onehot(jnp.where(valid, cell, -1), 192)
        label = jnp.zeros((WIN, 1), jnp.int32)
        label_t = jnp.zeros((1, WIN), jnp.int32)
        for i in range(6):
            band = bands[lax.rem(lat * 24 + shift_lat + (6 * w + i), ROWS)]
            label = jnp.where(row == i, band, label)
            label_t = jnp.where(row_t == i, band, label_t)
        free = jnp.where(valid, 0, 1)
        seen = jnp.where(valid_t, 1, 0)
        match = jnp.where(label == label_t, 1, 0)
        bias[w] = jnp.where(seen * (match + free) > 0, 0.0, MASKED)

    r = column(192)
    out_level = (r >= 96).astype(jnp.int32)
    frame_col = ((r - 96 * out_level) >> 3) - shift_lon
    left = frame_col < 0
    second = (frame_col >= 6).astype(jnp.int32)
    place = jnp.where(left, 160 + 6 + frame_col, HALF * second + frame_col - 6 * second)
    for b in range(3):
        frame_row = (r & 7) + (8 * b + 6) - shift_lat
        slot = (frame_row * 43) >> 8
        inner = 36 * out_level + 6 * (frame_row - 6 * slot)
        Po[b] = onehot(240 * (slot - b) + inner + place, 720)

    ring(3)

    sk = [
        remote(E.at[0:144], E.at[576:720], sk_send.at[0], sk_recv.at[0], at(lat, lon_prev)),
        remote(E.at[288:432], E.at[720:864], sk_send.at[1], sk_recv.at[1], at(lat, lon_prev)),
        remote(Sp, E.at[864:1056], sk_send.at[2], sk_recv.at[2], at(lat_prev, lon)),
        remote(Sp.at[0:96], E.at[1056:1152], sk_send.at[3], sk_recv.at[3], at(lat_prev, lon_prev)),
    ]
    for copy in sk:
        copy.start()

    w4x.wait_recv()
    w4r = remote(W4.at[128:192], W4.at[192:256], w4_send.at[2], w4_recv.at[2], sibling)
    w4r.start()
    wr = [
        remote(Wb.at[2, rows(j)], Wb.at[3, rows(j)], wr_send.at[j], wr_recv.at[j], sibling) for j in (0, 2, 1, 3)
    ]
    for arrived, onward in zip(wx, wr):
        arrived.wait_recv()
        onward.start()

    ring(4)

    @pl.when(is_home)
    def _():
        k = lax.rem(z, 4) * 2 + (1 - c)
        remote(xs, G.at[k], own_send.at[2], ring_recv.at[k], sibling).wait_recv()

    for w in range(2):
        tails = G[4 * w : 4 * w + 4, 128:144, :].reshape(64, 512)
        for f in range(4):
            pick = onehot((i16 >> 2) * 16 + 4 * f + (i16 & 3), 64)
            Xt[16 * w : 16 * w + 16, 512 * f : 512 * f + 512] = dot(pick, tails).astype(BF)

    loads[2].wait()
    ws.wait_recv()
    for copy in wr:
        copy.wait_recv()
    w4s.wait_recv()
    w4r.wait_recv()

    for h in range(4):
        main = jnp.zeros((256, 192), F32)
        for f in range(4):
            main = main + dot_nt(
                G[:, 32 * f : 32 * f + 32, :].reshape(256, 512), Wb[h, :, 512 * f : 512 * f + 512]
            )
        tail = dot_nt(Xt[...], Wb[h])
        for w in range(2):
            PK[h, w, 0:128, :] = main[128 * w : 128 * w + 128].astype(BF)
            PK[h, w, 128:144, :] = tail[16 * w : 16 * w + 16].astype(BF)

    i64 = column(64)
    for w in range(2):
        terms = jnp.zeros((144, 512), F32)
        for h in range(4):
            packed = PK[h, w]
            mixed = softmax_mix(packed[:, 0:64], packed[:, 64:128], packed[:, 128:192], None).astype(BF)
            terms = terms + dot(mixed, W4[64 * h : 64 * h + 64, :])
        terms = terms.astype(BF)
        tails = jnp.zeros((64, 128), F32)
        for f in range(4):
            part = terms[:, 128 * f : 128 * f + 128]
            for q in range(4):
                msg[4 * w + q, 32 * f : 32 * f + 32, :] = part[32 * q : 32 * q + 32]
            tails = tails + dot(
                onehot(jnp.where(((i64 >> 2) & 3) == f, (i64 >> 4) * 4 + (i64 & 3), -1), 16), part[128:144]
            )
        tails = tails.astype(BF)
        for q in range(4):
            msg[4 * w + q, 128:144, :] = tails[16 * q : 16 * q + 16]

    def term(k):
        return remote(msg.at[k], R.at[z], aa_send.at[k], aa_recv.at[z], at(lat, base + 8 * c + k))

    for k in range(8):

        @pl.when(base + 8 * c + k != lon)
        def _(k=k):
            term(k).start()

    @pl.when(is_home)
    def _():
        R[pl.ds(z, 1)] = msg[pl.ds(mine, 1)]

    total = jnp.zeros((144, 128), F32)
    for s in range(8):

        @pl.when(base + 2 * s + target != lon)
        def _(s=s):
            remote(msg.at[0], R.at[s], aa_send.at[0], aa_recv.at[s], sibling).wait_recv()

    for s in range(8):
        total = total + R[s].astype(F32)
    for f in range(4):
        lanes = slice(128 * f, 128 * f + 128)
        LE[0:32, lanes] = (cup[0:32, lanes] + total[32 * f : 32 * f + 32]).astype(BF)
        pick = jnp.where(
            (lax.broadcasted_iota(jnp.int32, (16, 16), 1) == 4 * f + i16) & (i16 < 4), 1.0, 0.0
        )
        rest = jnp.dot(pick, total[128:144], preferred_element_type=F32, precision=lax.Precision.HIGHEST)
        LE[32:48, lanes] = (cup[32:48, lanes] + rest).astype(BF)

    li = [
        remote(LE.at[0:48], LE.at[48:96], li_send.at[0], li_recv.at[0], at(lat, lon_prev)),
        remote(LE.at[0:48], LE.at[96:144], li_send.at[1], li_recv.at[1], at(lat_prev, lon)),
        remote(LE.at[0:48], LE.at[144:192], li_send.at[2], li_recv.at[2], at(lat_prev, lon_prev)),
    ]
    for copy in li:
        copy.start()

    for copy in sk:
        copy.wait_recv()
    for w in range(4):
        source_row = row + (shift_lat + 6 * w)
        cell = jnp.where(
            source_col < 12,
            288 * level + 24 * source_col + source_row,
            576 + 144 * level + 24 * (source_col - 12) + source_row,
        )
        below = 864 + 16 * source_col + 8 * level + source_row - 24
        cell = jnp.where(source_row < 24, cell, below)
        width = 1152 if w == 3 else 864
        skF[w] = dot(onehot(jnp.where(valid, cell, -1), width), E[0:width, :]).astype(BF)

    for load in loads[4:]:
        load.wait()
    for copy in li:
        copy.wait_recv()

    def window(t, carry):
        w = lax.rem(t + 3, 4)
        stream = skF[w].astype(F32) + dot(Pl[w], LE[...])
        pk1[...] = dot(normalize(stream).astype(BF), w1v[...]).astype(BF)
        allowed = bias[w]
        for pair in range(4):
            both = []
            for h in (2 * pair, 2 * pair + 1):
                q = pk1[:, 192 * h : 192 * h + 64]
                k = pk1[:, 192 * h + 64 : 192 * h + 128]
                v = pk1[:, 192 * h + 128 : 192 * h + 192]
                both.append(softmax_mix(q, k, v, allowed))
            mix[:, 128 * pair : 128 * pair + 128] = jnp.concatenate(both, axis=1).astype(BF)
        attended = stream + dot(mix[...], wo1v[...])
        normed2 = normalize(attended).astype(BF)
        result = attended
        for f in range(2):
            hidden = jax.nn.gelu(dot(normed2, wiv[:, 1024 * f : 1024 * f + 1024])).astype(BF)
            result = result + dot(hidden, wfv[1024 * f : 1024 * f + 1024, :])
        Z[w + 1, 0:WIN, :] = result.astype(BF)
        to_lon(w).start()

        @pl.when(t == 0)
        def _():
            to_lat.start()
            to_both.start()

        return carry

    def to_lon(w):
        return remote(
            Z.at[w + 1, HALF:WIN], Z.at[w + 1, WIN : WIN + HALF], lo_send.at[w], lo_recv.at[w], at(lat, lon_next)
        )

    to_lat = remote(Z.at[4, 0:WIN], Z.at[0, 0:WIN], la_send.at[0], la_recv.at[0], at(lat_next, lon))
    to_both = remote(
        Z.at[4, HALF:WIN], Z.at[0, WIN : WIN + HALF], la_send.at[1], la_recv.at[1], at(lat_next, lon_next)
    )
    lax.fori_loop(0, 4, window, 0)

    to_lat.wait_recv()
    to_both.wait_recv()
    for w in (3, 0, 1, 2):
        to_lon(w).wait_recv()
    for b in range(3):
        taken = dot(Po[b, :, 0:240], Z[b]) + dot(Po[b, :, 240:480], Z[b + 1]) + dot(Po[b, :, 480:720], Z[b + 2])
        out[:, 8 * b : 8 * b + 8, :] = taken.astype(BF).reshape(24, 8, D1)

    for copy in [*own, *wx, ws, w4x, w4s, w4r, *wr, *sk, *li, to_lat, to_both]:
        copy.wait_send()

    @pl.when(jnp.logical_not(is_home))
    def _():
        own_sib.wait_send()

    for s in (1, 2, 3):
        for way, k, here, onward in ring_steps(s):
            if onward:

                @pl.when(here)
                def _(way=way, k=k):
                    relay(k, way).wait_send()

    for k in range(8):

        @pl.when(base + 8 * c + k != lon)
        def _(k=k):
            term(k).wait_send()

    for w in range(4):
        to_lon(w).wait_send()


def local(
    skip,
    coarse,
    offsets,
    bands,
    qkv3_weight,
    out3_weight,
    up_weight,
    qkv1_weight,
    out1_weight,
    mlp_in,
    mlp_out,
):
    cells = jnp.transpose(coarse, (1, 2, 0, 3)).reshape(CELLS3 // 2, 2, D3)
    vmem = pl.BlockSpec(memory_space=pltpu.VMEM)
    smem = pl.BlockSpec(memory_space=pltpu.SMEM)
    hbm = pl.BlockSpec(memory_space=ANY)
    dma = pltpu.SemaphoreType.DMA
    placed = pl.pallas_call(
        kernel,
        out_shape=jax.ShapeDtypeStruct((24, 24, D1), BF),
        in_specs=[smem, smem, vmem] + [hbm] * 8,
        out_specs=vmem,
        scratch_shapes=[
            pltpu.VMEM((144, 512), BF),
            pltpu.VMEM((8, 144, 512), BF),
            pltpu.VMEM((4, 192, D3), BF),
            pltpu.VMEM((64, D3), BF),
            pltpu.VMEM((D3, D1), BF),
            pltpu.VMEM((256, D1), BF),
            pltpu.VMEM((48, D1), F32),
            pltpu.VMEM((192, D1), BF),
            pltpu.VMEM((1152, D1), BF),
            pltpu.VMEM((4, WIN, D1), BF),
            pltpu.VMEM((4, WIN, WIN), F32),
            pltpu.VMEM((4, WIN, 192), BF),
            pltpu.VMEM((3, 192, 720), BF),
            pltpu.VMEM((32, D3), BF),
            pltpu.VMEM((4, 2, 144, 192), BF),
            pltpu.VMEM((8, 144, 128), BF),
            pltpu.VMEM((8, 144, 128), BF),
            pltpu.VMEM((192, D1), BF),
            pltpu.VMEM((D1, 3 * D1), BF),
            pltpu.VMEM((D1, D1), BF),
            pltpu.VMEM((D1, FF), BF),
            pltpu.VMEM((FF, D1), BF),
            pltpu.VMEM((WIN, 3 * D1), BF),
            pltpu.VMEM((WIN, D1), BF),
            pltpu.VMEM((5, 240, D1), BF),
            dma((8,)),
            dma((3,)),
            dma((8, 2)),
            dma((8,)),
            dma((4,)),
            dma((4,)),
            dma((1,)),
            dma((1,)),
            dma((4,)),
            dma((4,)),
            dma((3,)),
            dma((3,)),
            dma((4,)),
            dma((4,)),
            dma((8,)),
            dma((8,)),
            dma((3,)),
            dma((3,)),
            dma((4,)),
            dma((4,)),
            dma((2,)),
            dma((2,)),
        ],
        compiler_params=pltpu.CompilerParams(
            collective_id=0, has_side_effects=True, vmem_limit_bytes=56 * 1024 * 1024
        ),
    )(
        offsets,
        bands,
        cells,
        jnp.transpose(skip, (0, 2, 1, 3)).reshape(OWN, D1),
        qkv3_weight.T,
        out3_weight,
        up_weight,
        qkv1_weight,
        out1_weight,
        mlp_in,
        mlp_out,
    )
    return jnp.transpose(placed.reshape(2, 12, 24, D1), (0, 2, 1, 3))


def solution(mesh):
    return jax.shard_map(
        local,
        mesh=mesh,
        in_specs=(
            P(None, "lat", "lon", None),
            P(None, "lat", "lon", None),
            P(),
            P(),
            P(None, "lon"),
            P("lon", None),
            P(),
            P(),
            P(),
            P(),
            P(),
        ),
        out_specs=P(None, "lat", "lon", None),
        check_vma=False,
    )
```

```python
import jax
import jax.numpy as jnp
from jax import lax
from jax.experimental import pallas as pl
from jax.experimental.pallas import tpu as pltpu
from jax.sharding import PartitionSpec as P

LATS = 8
LONS = 32
ROWS = 192
D3 = 2048
D1 = 512
FF = 2048
HEAD = 64
CELLS3 = 36
OWN = 576
SCALE = HEAD**-0.5
EPS = 1e-05
HALF = 80
WIN = 2 * HALF
MASKED = -1e30

F32 = jnp.float32
BF = jnp.bfloat16
MESH = pl.DeviceIdType.MESH
ANY = pl.ANY


def dot(a, b):
    return jnp.dot(a, b, preferred_element_type=F32)


def dot_nt(a, b):
    return lax.dot_general(a, b, (((1,), (1,)), ((), ())), preferred_element_type=F32)


def normalize(values):
    centred = values - jnp.mean(values, axis=-1, keepdims=True)
    spread = jnp.mean(centred * centred, axis=-1, keepdims=True)
    return centred * lax.rsqrt(spread + EPS)


def column(n):
    return lax.broadcasted_iota(jnp.int32, (n, 1), 0)


def onehot(target, width):
    n = target.shape[0]
    hit = lax.broadcasted_iota(jnp.int32, (n, width), 1) == target
    return jnp.where(hit, 1.0, 0.0).astype(BF)


def frame_cell(n):
    half = (n >= HALF).astype(jnp.int32)
    m = n - HALF * half
    valid = m < 72
    sixth = (m * 43) >> 8
    return valid, sixth & 1, 5 - (sixth >> 1), m - 6 * sixth + 6 * half


def softmax_mix(q, k, v, bias):
    scores = dot_nt(q, k) * SCALE
    if bias is not None:
        scores = scores + bias
    weights = jnp.exp(scores - jnp.max(scores, axis=1, keepdims=True))
    total = jnp.sum(weights, axis=1, keepdims=True)
    return dot(weights.astype(BF), v) * (1.0 / total)


def kernel(
    offs,
    bands,
    coarse,
    skip,
    wq,
    wo,
    up,
    w1,
    wo1,
    wi,
    wf,
    out,
    xs,
    G,
    Wb,
    wov,
    upv,
    W4,
    cup,
    Sp,
    E,
    skF,
    bias,
    Pl,
    Po,
    Xt,
    PK,
    msg,
    R,
    LE,
    w1v,
    wo1v,
    wiv,
    wfv,
    pk1,
    mix,
    Z,
    loc,
    own_send,
    ring_send,
    ring_recv,
    wx_send,
    wx_recv,
    ws_send,
    ws_recv,
    wr_send,
    wr_recv,
    w4_send,
    w4_recv,
    sk_send,
    sk_recv,
    aa_send,
    aa_recv,
    li_send,
    li_recv,
    lo_send,
    lo_recv,
    la_send,
    la_recv,
):
    lat = lax.axis_index("lat")
    lon = lax.axis_index("lon")
    xl = lon // 16
    z = lax.rem(lon // 2, 8)
    c = lax.rem(lon, 2)
    base = xl * 16

    def at(lat_, lon_):
        return {"lat": lat_, "lon": lon_}

    def chip(z_, c_):
        return at(lat, base + 2 * lax.rem(z_ + 8, 8) + c_)

    sibling = at(lat, lon + 1 - 2 * c)
    across = lax.rem(lon + 16, 32)
    near = at(lat, across)
    far = at(lat + 1 - 2 * lax.rem(lat, 2), across)
    lon_next = lax.rem(lon + 1, LONS)
    lon_prev = lax.rem(lon + LONS - 1, LONS)
    lat_next = lax.rem(lat + 1, LATS)
    lat_prev = lax.rem(lat + LATS - 1, LATS)

    def remote(src, dst, send, recv, device):
        return pltpu.make_async_remote_copy(
            src_ref=src, dst_ref=dst, send_sem=send, recv_sem=recv, device_id=device, device_id_type=MESH
        )

    loads = [
        pltpu.make_async_copy(src, dst, loc.at[i])
        for i, (src, dst) in enumerate(
            [(up, upv), (wo, wov), (wq, Wb.at[0]), (skip, E.at[0:OWN]), (w1, w1v), (wo1, wo1v), (wi, wiv), (wf, wfv)]
        )
    ]
    for load in loads:
        load.start()

    barrier = pltpu.get_barrier_semaphore()
    greeted = [chip(z + d, c_) for d in range(1, 8) for c_ in (0, 1)] + [
        sibling,
        near,
        far,
        at(lat, lon_next),
        at(lat, lon_prev),
        at(lat_next, lon),
        at(lat_prev, lon),
        at(lat_next, lon_next),
        at(lat_prev, lon_prev),
    ]
    for device in greeted:
        pl.semaphore_signal(barrier, inc=1, device_id=device, device_id_type=MESH)

    cells = coarse[...].astype(F32).reshape(CELLS3, D3)
    cells = jnp.concatenate([cells, jnp.zeros((12, D3), F32)], axis=0)
    normed3 = normalize(cells).astype(BF)
    cells = cells.astype(BF)
    rest = jnp.zeros((16, 512), F32)
    i16 = column(16)
    for f in range(4):
        part = normed3[:, 512 * f : 512 * f + 512]
        xs[32 * f : 32 * f + 32, :] = part[0:32]
        pick = onehot(jnp.where((i16 >> 2) == f, i16 & 3, -1), 16)
        rest = rest + dot(pick, part[32:48])
    xs[128:144, :] = rest.astype(BF)

    for first in (64, 144, 224):
        Z[0, first : first + 16, :] = jnp.zeros((16, D1), BF)

    pl.semaphore_wait(barrier, len(greeted))

    target = z // 4
    mine = lax.rem(z, 4) * 2 + c
    is_home = target == c
    own = [
        remote(xs, G.at[mine], own_send.at[0], ring_recv.at[mine], chip(z + 1, target)),
        remote(xs, G.at[mine], own_send.at[1], ring_recv.at[mine], chip(z - 1, target)),
    ]
    own_sib = remote(xs, G.at[mine], own_send.at[2], ring_recv.at[mine], sibling)
    for copy in own:
        copy.start()

    @pl.when(jnp.logical_not(is_home))
    def _():
        own_sib.start()

    def rows(j):
        return pl.ds(48 * j, 48)

    wx = [
        remote(wq.at[rows(j)], Wb.at[2, rows(j)], wx_send.at[j], wx_recv.at[j], near if j < 2 else far)
        for j in (0, 2, 1, 3)
    ]
    for copy in wx:
        copy.start()
    ws = remote(wq, Wb.at[1], ws_send.at[0], ws_recv.at[0], sibling)
    ws.start()

    loads[0].wait()
    loads[1].wait()
    W4[0:64, :] = dot(wov[...], upv[...]).astype(BF)
    w4x = remote(W4.at[0:64], W4.at[128:192], w4_send.at[0], w4_recv.at[0], near)
    w4x.start()
    w4s = remote(W4.at[0:64], W4.at[64:128], w4_send.at[1], w4_recv.at[1], sibling)
    w4s.start()
    cup[...] = dot(cells, upv[...])

    @pl.when(is_home)
    def _():
        G[pl.ds(mine, 1)] = xs[...].reshape(1, 144, 512)

    def relay(k, way):
        return remote(
            G.at[k], G.at[k], ring_send.at[k, way], ring_recv.at[k], chip(z + (1 if way == 0 else -1), c)
        )

    def ring_steps(s):
        for way in (0, 1):
            source = lax.rem(z + (8 - s if way == 0 else s), 8)
            for core in (0, 1):
                limit = 4 if core == way else 3
                if s <= limit:
                    yield way, lax.rem(source, 4) * 2 + core, source // 4 == c, s < limit

    def ring(s):
        for way, k, here, onward in ring_steps(s):

            @pl.when(here)
            def _(way=way, k=k, onward=onward):
                copy = relay(k, way)
                copy.wait_recv()
                if onward:
                    copy.start()

    loads[3].wait()
    r128 = column(128)
    r64 = r128 & 63
    ten = (r64 * 103) >> 10
    five = (r64 * 205) >> 10
    first_rows = (five & 1) * 288 + (ten + 6 * (r128 >> 6)) * 24 + r64 - 5 * five
    Sp[...] = dot(onehot(jnp.where(r64 < 60, first_rows, -1), OWN), E[0:OWN, :]).astype(BF)

    sk_lat = remote(Sp, E.at[864:992], sk_send.at[2], sk_recv.at[2], at(lat_prev, lon))
    sk_lat.start()

    ring(1)

    a = offs[0]
    shift_lat = jnp.where(a >= 6, a - 6, a)
    shift_lon = offs[1]
    n = column(WIN)
    valid, level, row, col = frame_cell(n)
    valid_t, _, row_t, _ = frame_cell(lax.broadcasted_iota(jnp.int32, (1, WIN), 1))
    source_col = col + shift_lon
    r = column(192)
    out_level = (r >= 96).astype(jnp.int32)
    frame_col = ((r - 96 * out_level) >> 3) - shift_lon
    left = frame_col < 0
    second = (frame_col >= 6).astype(jnp.int32)
    place = jnp.where(left, 160 + 6 + frame_col, HALF * second + frame_col - 6 * second)
    for b in range(3):
        frame_row = (r & 7) + (8 * b + 6) - shift_lat
        slot = (frame_row * 43) >> 8
        inner = 12 * (5 - (frame_row - 6 * slot)) + 6 * out_level
        Po[b] = onehot(240 * (slot - b) + inner + place, 720)

    ring(2)

    ring(3)

    sk_lon = [
        remote(E.at[0:144], E.at[576:720], sk_send.at[0], sk_recv.at[0], at(lat, lon_prev)),
        remote(E.at[288:432], E.at[720:864], sk_send.at[1], sk_recv.at[1], at(lat, lon_prev)),
    ]
    for copy in sk_lon:
        copy.start()

    w4x.wait_recv()
    w4r = remote(W4.at[128:192], W4.at[192:256], w4_send.at[2], w4_recv.at[2], sibling)
    w4r.start()
    wr = [
        remote(Wb.at[2, rows(j)], Wb.at[3, rows(j)], wr_send.at[j], wr_recv.at[j], sibling) for j in (0, 2, 1, 3)
    ]
    for arrived, onward in zip(wx, wr):
        arrived.wait_recv()
        onward.start()

    for w in range(4):
        source_row = row + (shift_lat + 6 * w)
        coarse_row = source_row >> 2
        coarse_col = source_col >> 2
        row_out = (coarse_row >= 6).astype(jnp.int32)
        col_out = (coarse_col >= 3).astype(jnp.int32)
        cell = 48 * col_out + row_out * (96 - 32 * col_out) + level + 6 * (coarse_row - 6 * row_out) + 2 * (coarse_col - 3 * col_out)
        Pl[w] = onehot(jnp.where(valid, cell, -1), 128)
        label = jnp.zeros((WIN, 1), jnp.int32)
        label_t = jnp.zeros((1, WIN), jnp.int32)
        for i in range(6):
            band = bands[lax.rem(lat * 24 + shift_lat + (6 * w + i), ROWS)]
            label = jnp.where(row == i, band, label)
            label_t = jnp.where(row_t == i, band, label_t)
        free = jnp.where(valid, 0, 1)
        seen = jnp.where(valid_t, 1, 0)
        match = jnp.where(label == label_t, 1, 0)
        bias[w] = jnp.where(seen * (match + free) > 0, 0.0, MASKED)

    sk_lat.wait_recv()
    sk_both = remote(E.at[864:928], E.at[992:1056], sk_send.at[3], sk_recv.at[3], at(lat, lon_prev))
    sk_both.start()

    ring(4)

    @pl.when(is_home)
    def _():
        k = lax.rem(z, 4) * 2 + (1 - c)
        remote(xs, G.at[k], own_send.at[2], ring_recv.at[k], sibling).wait_recv()

    for w in range(2):
        tails = G[4 * w : 4 * w + 4, 128:144, :].reshape(64, 512)
        for f in range(4):
            pick = onehot((i16 >> 2) * 16 + 4 * f + (i16 & 3), 64)
            Xt[16 * w : 16 * w + 16, 512 * f : 512 * f + 512] = dot(pick, tails).astype(BF)

    loads[2].wait()
    ws.wait_recv()
    for copy in wr:
        copy.wait_recv()
    w4s.wait_recv()
    w4r.wait_recv()

    for h in range(4):
        main = jnp.zeros((256, 192), F32)
        for f in range(4):
            main = main + dot_nt(
                G[:, 32 * f : 32 * f + 32, :].reshape(256, 512), Wb[h, :, 512 * f : 512 * f + 512]
            )
        tail = dot_nt(Xt[...], Wb[h])
        for w in range(2):
            PK[h, w, 0:128, :] = main[128 * w : 128 * w + 128].astype(BF)
            PK[h, w, 128:144, :] = tail[16 * w : 16 * w + 16].astype(BF)

    def term(k):
        return remote(msg.at[k], R.at[z], aa_send.at[k], aa_recv.at[z], at(lat, base + 8 * c + k))

    i64 = column(64)
    for w in range(2):
        terms = jnp.zeros((144, 512), F32)
        for h in range(4):
            packed = PK[h, w]
            mixed = softmax_mix(packed[:, 0:64], packed[:, 64:128], packed[:, 128:192], None).astype(BF)
            terms = terms + dot(mixed, W4[64 * h : 64 * h + 64, :])
        terms = terms.astype(BF)
        tails = jnp.zeros((64, 128), F32)
        for f in range(4):
            part = terms[:, 128 * f : 128 * f + 128]
            for q in range(4):
                msg[4 * w + q, 32 * f : 32 * f + 32, :] = part[32 * q : 32 * q + 32]
            tails = tails + dot(
                onehot(jnp.where(((i64 >> 2) & 3) == f, (i64 >> 4) * 4 + (i64 & 3), -1), 16), part[128:144]
            )
        tails = tails.astype(BF)
        for q in range(4):
            msg[4 * w + q, 128:144, :] = tails[16 * q : 16 * q + 16]
        for k in range(4 * w, 4 * w + 4):

            @pl.when(base + 8 * c + k != lon)
            def _(k=k):
                term(k).start()


    @pl.when(is_home)
    def _():
        R[pl.ds(z, 1)] = msg[pl.ds(mine, 1)]

    for copy in sk_lon:
        copy.wait_recv()
    sk_both.wait_recv()
    for w in range(4):
        source_row = row + (shift_lat + 6 * w)
        cell = jnp.where(
            source_col < 12,
            288 * level + 24 * source_col + source_row,
            576 + 144 * level + 24 * (source_col - 12) + source_row,
        )
        third = (source_col >= 6).astype(jnp.int32) + (source_col >= 12).astype(jnp.int32)
        below = 864 + 64 * third + 10 * (source_col - 6 * third) + 5 * level + source_row - 24
        cell = jnp.where(source_row < 24, cell, below)
        width = 1056 if w == 3 else 864
        skF[w] = dot(onehot(jnp.where(valid, cell, -1), width), E[0:width, :]).astype(BF)

    total = jnp.zeros((144, 128), F32)
    for s in range(8):

        @pl.when(base + 2 * s + target != lon)
        def _(s=s):
            remote(msg.at[0], R.at[s], aa_send.at[0], aa_recv.at[s], sibling).wait_recv()

    for s in range(8):
        total = total + R[s].astype(F32)
    for f in range(4):
        lanes = slice(128 * f, 128 * f + 128)
        LE[0:32, lanes] = (cup[0:32, lanes] + total[32 * f : 32 * f + 32]).astype(BF)
        pick = jnp.where(
            (lax.broadcasted_iota(jnp.int32, (16, 16), 1) == 4 * f + i16) & (i16 < 4), 1.0, 0.0
        )
        rest = jnp.dot(pick, total[128:144], preferred_element_type=F32, precision=lax.Precision.HIGHEST)
        LE[32:48, lanes] = (cup[32:48, lanes] + rest).astype(BF)

    li_lon = remote(LE.at[0:48], LE.at[48:96], li_send.at[0], li_recv.at[0], at(lat, lon_prev))
    li_lat = remote(LE.at[0:16], LE.at[96:112], li_send.at[1], li_recv.at[1], at(lat_prev, lon))
    li_both = remote(LE.at[0:16], LE.at[112:128], li_send.at[2], li_recv.at[2], at(lat_prev, lon_prev))
    li = [li_both, li_lat, li_lon]
    for copy in li:
        copy.start()

    for load in loads[4:]:
        load.wait()
    for copy in li:
        copy.wait_recv()

    def window(t, carry):
        w = lax.rem(t + 3, 4)
        stream = skF[w].astype(F32) + dot(Pl[w], LE[...])
        pk1[...] = dot(normalize(stream).astype(BF), w1v[...]).astype(BF)
        allowed = bias[w]
        for pair in range(4):
            both = []
            for h in (2 * pair, 2 * pair + 1):
                q = pk1[:, 192 * h : 192 * h + 64]
                k = pk1[:, 192 * h + 64 : 192 * h + 128]
                v = pk1[:, 192 * h + 128 : 192 * h + 192]
                both.append(softmax_mix(q, k, v, allowed))
            mix[:, 128 * pair : 128 * pair + 128] = jnp.concatenate(both, axis=1).astype(BF)
        attended = stream + dot(mix[...], wo1v[...])
        normed2 = normalize(attended).astype(BF)
        result = attended
        for f in range(2):
            hidden = jax.nn.gelu(dot(normed2, wiv[:, 1024 * f : 1024 * f + 1024])).astype(BF)
            result = result + dot(hidden, wfv[1024 * f : 1024 * f + 1024, :])
        Z[w + 1, 0:WIN, :] = result.astype(BF)
        to_lon(w).start()

        @pl.when(t == 0)
        def _():
            to_lat[0].start()
            to_lat[1].start()

        return carry

    def to_lon(w):
        return remote(
            Z.at[w + 1, HALF:WIN], Z.at[w + 1, WIN : WIN + HALF], lo_send.at[w], lo_recv.at[w], at(lat, lon_next)
        )

    to_lat = [
        remote(Z.at[4, 80:144], Z.at[0, 80:144], la_send.at[1], la_recv.at[1], at(lat_next, lon)),
        remote(Z.at[4, 0:64], Z.at[0, 0:64], la_send.at[0], la_recv.at[0], at(lat_next, lon)),
    ]
    to_both = remote(Z.at[0, 80:144], Z.at[0, 160:224], la_send.at[2], la_recv.at[2], at(lat, lon_next))
    lax.fori_loop(0, 4, window, 0)

    to_lat[0].wait_recv()
    to_both.start()
    to_lat[1].wait_recv()
    to_both.wait_recv()
    for w in (3, 0, 1, 2):
        to_lon(w).wait_recv()
    for b in range(3):
        taken = dot(Po[b, :, 0:240], Z[b]) + dot(Po[b, :, 240:480], Z[b + 1]) + dot(Po[b, :, 480:720], Z[b + 2])
        out[:, 8 * b : 8 * b + 8, :] = taken.astype(BF).reshape(24, 8, D1)

    for copy in [*own, *wx, ws, w4x, w4s, w4r, *wr, sk_lat, *sk_lon, sk_both, *li, *to_lat, to_both]:
        copy.wait_send()

    @pl.when(jnp.logical_not(is_home))
    def _():
        own_sib.wait_send()

    for s in (1, 2, 3):
        for way, k, here, onward in ring_steps(s):
            if onward:

                @pl.when(here)
                def _(way=way, k=k):
                    relay(k, way).wait_send()

    for k in range(8):

        @pl.when(base + 8 * c + k != lon)
        def _(k=k):
            term(k).wait_send()

    for w in range(4):
        to_lon(w).wait_send()


def local(
    skip,
    coarse,
    offsets,
    bands,
    qkv3_weight,
    out3_weight,
    up_weight,
    qkv1_weight,
    out1_weight,
    mlp_in,
    mlp_out,
):
    cells = jnp.transpose(coarse, (1, 2, 0, 3)).reshape(CELLS3 // 2, 2, D3)
    vmem = pl.BlockSpec(memory_space=pltpu.VMEM)
    smem = pl.BlockSpec(memory_space=pltpu.SMEM)
    hbm = pl.BlockSpec(memory_space=ANY)
    dma = pltpu.SemaphoreType.DMA
    placed = pl.pallas_call(
        kernel,
        out_shape=jax.ShapeDtypeStruct((24, 24, D1), BF),
        in_specs=[smem, smem, vmem] + [hbm] * 8,
        out_specs=vmem,
        scratch_shapes=[
            pltpu.VMEM((144, 512), BF),
            pltpu.VMEM((8, 144, 512), BF),
            pltpu.VMEM((4, 192, D3), BF),
            pltpu.VMEM((64, D3), BF),
            pltpu.VMEM((D3, D1), BF),
            pltpu.VMEM((256, D1), BF),
            pltpu.VMEM((48, D1), F32),
            pltpu.VMEM((128, D1), BF),
            pltpu.VMEM((1056, D1), BF),
            pltpu.VMEM((4, WIN, D1), BF),
            pltpu.VMEM((4, WIN, WIN), F32),
            pltpu.VMEM((4, WIN, 128), BF),
            pltpu.VMEM((3, 192, 720), BF),
            pltpu.VMEM((32, D3), BF),
            pltpu.VMEM((4, 2, 144, 192), BF),
            pltpu.VMEM((8, 144, 128), BF),
            pltpu.VMEM((8, 144, 128), BF),
            pltpu.VMEM((128, D1), BF),
            pltpu.VMEM((D1, 3 * D1), BF),
            pltpu.VMEM((D1, D1), BF),
            pltpu.VMEM((D1, FF), BF),
            pltpu.VMEM((FF, D1), BF),
            pltpu.VMEM((WIN, 3 * D1), BF),
            pltpu.VMEM((WIN, D1), BF),
            pltpu.VMEM((5, 240, D1), BF),
            dma((8,)),
            dma((3,)),
            dma((8, 2)),
            dma((8,)),
            dma((4,)),
            dma((4,)),
            dma((1,)),
            dma((1,)),
            dma((4,)),
            dma((4,)),
            dma((3,)),
            dma((3,)),
            dma((4,)),
            dma((4,)),
            dma((8,)),
            dma((8,)),
            dma((3,)),
            dma((3,)),
            dma((4,)),
            dma((4,)),
            dma((3,)),
            dma((3,)),
        ],
        compiler_params=pltpu.CompilerParams(
            collective_id=0, has_side_effects=True, vmem_limit_bytes=56 * 1024 * 1024
        ),
    )(
        offsets,
        bands,
        cells,
        jnp.transpose(skip, (0, 2, 1, 3)).reshape(OWN, D1),
        qkv3_weight.T,
        out3_weight,
        up_weight,
        qkv1_weight,
        out1_weight,
        mlp_in,
        mlp_out,
    )
    return jnp.transpose(placed.reshape(2, 12, 24, D1), (0, 2, 1, 3))


def solution(mesh):
    return jax.shard_map(
        local,
        mesh=mesh,
        in_specs=(
            P(None, "lat", "lon", None),
            P(None, "lat", "lon", None),
            P(),
            P(),
            P(None, "lon"),
            P("lon", None),
            P(),
            P(),
            P(),
            P(),
            P(),
        ),
        out_specs=P(None, "lat", "lon", None),
        check_vma=False,
    )
```

```python
import jax
import jax.numpy as jnp
from jax import lax
from jax.experimental import pallas as pl
from jax.experimental.pallas import tpu as pltpu
from jax.sharding import PartitionSpec as P

LATS = 8
LONS = 32
ROWS = 192
D3 = 2048
D1 = 512
FF = 2048
HEAD = 64
CELLS3 = 36
OWN = 576
PIECES = 3
PIECE = 144 // PIECES
SCALE = HEAD**-0.5
EPS = 1e-05
HALF = 80
WIN = 2 * HALF
MASKED = -1e30

F32 = jnp.float32
BF = jnp.bfloat16
MESH = pl.DeviceIdType.MESH
ANY = pl.ANY


def dot(a, b):
    return jnp.dot(a, b, preferred_element_type=F32)


def dot_nt(a, b):
    return lax.dot_general(a, b, (((1,), (1,)), ((), ())), preferred_element_type=F32)


def normalize(values):
    centred = values - jnp.mean(values, axis=-1, keepdims=True)
    spread = jnp.mean(centred * centred, axis=-1, keepdims=True)
    return centred * lax.rsqrt(spread + EPS)


def column(n):
    return lax.broadcasted_iota(jnp.int32, (n, 1), 0)


def onehot(target, width):
    n = target.shape[0]
    hit = lax.broadcasted_iota(jnp.int32, (n, width), 1) == target
    return jnp.where(hit, 1.0, 0.0).astype(BF)


def frame_cell(n):
    half = (n >= HALF).astype(jnp.int32)
    m = n - HALF * half
    valid = m < 72
    sixth = (m * 43) >> 8
    return valid, sixth & 1, 5 - (sixth >> 1), m - 6 * sixth + 6 * half


def softmax_mix(q, k, v, bias):
    scores = dot_nt(q, k) * SCALE
    if bias is not None:
        scores = scores + bias
    weights = jnp.exp(scores - jnp.max(scores, axis=1, keepdims=True))
    total = jnp.sum(weights, axis=1, keepdims=True)
    return dot(weights.astype(BF), v) * (1.0 / total)


def kernel(
    offs,
    bands,
    coarse,
    skip,
    wq,
    wo,
    up,
    w1,
    wo1,
    wi,
    wf,
    out,
    xs,
    G,
    Wb,
    wov,
    upv,
    W4,
    cup,
    Sp,
    E,
    skF,
    bias,
    Pl,
    Po,
    Xt,
    PK,
    msg,
    R,
    LE,
    w1v,
    wo1v,
    wiv,
    wfv,
    pk1,
    mix,
    AT,
    Z,
    loc,
    own_send,
    ring_send,
    ring_recv,
    wx_send,
    wx_recv,
    ws_send,
    ws_recv,
    wr_send,
    wr_recv,
    w4_send,
    w4_recv,
    sk_send,
    sk_recv,
    aa_send,
    aa_recv,
    li_send,
    li_recv,
    lo_send,
    lo_recv,
    la_send,
    la_recv,
):
    lat = lax.axis_index("lat")
    lon = lax.axis_index("lon")
    xl = lon // 16
    z = lax.rem(lon // 2, 8)
    c = lax.rem(lon, 2)
    base = xl * 16

    def at(lat_, lon_):
        return {"lat": lat_, "lon": lon_}

    def chip(z_, c_):
        return at(lat, base + 2 * lax.rem(z_ + 8, 8) + c_)

    sibling = at(lat, lon + 1 - 2 * c)
    across = lax.rem(lon + 16, 32)
    near = at(lat, across)
    far = at(lat + 1 - 2 * lax.rem(lat, 2), across)
    lon_next = lax.rem(lon + 1, LONS)
    lon_prev = lax.rem(lon + LONS - 1, LONS)
    lat_next = lax.rem(lat + 1, LATS)
    lat_prev = lax.rem(lat + LATS - 1, LATS)

    def remote(src, dst, send, recv, device):
        return pltpu.make_async_remote_copy(
            src_ref=src, dst_ref=dst, send_sem=send, recv_sem=recv, device_id=device, device_id_type=MESH
        )

    loads = [
        pltpu.make_async_copy(src, dst, loc.at[i])
        for i, (src, dst) in enumerate(
            [(up, upv), (wo, wov), (wq, Wb.at[0]), (skip, E.at[0:OWN]), (w1, w1v), (wo1, wo1v), (wi, wiv), (wf, wfv)]
        )
    ]
    for load in loads:
        load.start()

    barrier = pltpu.get_barrier_semaphore()
    greeted = [chip(z + d, c_) for d in range(1, 8) for c_ in (0, 1)] + [
        sibling,
        near,
        far,
        at(lat, lon_next),
        at(lat, lon_prev),
        at(lat_next, lon),
        at(lat_prev, lon),
        at(lat_next, lon_next),
        at(lat_prev, lon_prev),
    ]
    for device in greeted:
        pl.semaphore_signal(barrier, inc=1, device_id=device, device_id_type=MESH)

    cells = coarse[...].astype(F32).reshape(CELLS3, D3)
    cells = jnp.concatenate([cells, jnp.zeros((12, D3), F32)], axis=0)
    normed3 = normalize(cells).astype(BF)
    cells = cells.astype(BF)
    rest = jnp.zeros((16, 512), F32)
    i16 = column(16)
    for f in range(4):
        part = normed3[:, 512 * f : 512 * f + 512]
        xs[32 * f : 32 * f + 32, :] = part[0:32]
        pick = onehot(jnp.where((i16 >> 2) == f, i16 & 3, -1), 16)
        rest = rest + dot(pick, part[32:48])
    xs[128:144, :] = rest.astype(BF)

    for first in (64, 144, 224):
        Z[0, first : first + 16, :] = jnp.zeros((16, D1), BF)

    pl.semaphore_wait(barrier, len(greeted))

    target = z // 4
    mine = lax.rem(z, 4) * 2 + c
    is_home = target == c

    def piece(t):
        return pl.ds(PIECE * t, PIECE)

    own = [
        remote(
            xs.at[piece(t)],
            G.at[mine, piece(t)],
            own_send.at[2 * t + way],
            ring_recv.at[mine, t],
            chip(z + 1 - 2 * way, target),
        )
        for t in range(PIECES)
        for way in (0, 1)
    ]
    own_sib = remote(xs, G.at[mine], own_send.at[2 * PIECES], ring_recv.at[mine, 0], sibling)
    for copy in own:
        copy.start()

    @pl.when(jnp.logical_not(is_home))
    def _():
        own_sib.start()

    def rows(j):
        return pl.ds(48 * j, 48)

    wx = [
        remote(wq.at[rows(j)], Wb.at[2, rows(j)], wx_send.at[j], wx_recv.at[j], near if j < 2 else far)
        for j in (0, 2, 1, 3)
    ]
    for copy in wx:
        copy.start()
    ws = remote(wq, Wb.at[1], ws_send.at[0], ws_recv.at[0], sibling)
    ws.start()

    loads[0].wait()
    loads[1].wait()
    W4[0:64, :] = dot(wov[...], upv[...]).astype(BF)
    w4x = remote(W4.at[0:64], W4.at[128:192], w4_send.at[0], w4_recv.at[0], near)
    w4x.start()
    w4s = remote(W4.at[0:64], W4.at[64:128], w4_send.at[1], w4_recv.at[1], sibling)
    w4s.start()
    cup[...] = dot(cells, upv[...])

    @pl.when(is_home)
    def _():
        G[pl.ds(mine, 1)] = xs[...].reshape(1, 144, 512)

    def relay(k, way, rows_, t):
        block = G.at[k, rows_]
        return remote(block, block, ring_send.at[k, way], ring_recv.at[k, t], chip(z + 1 - 2 * way, c))

    def ring_steps(s):
        for way in (0, 1):
            source = lax.rem(z + (8 - s if way == 0 else s), 8)
            for core in (0, 1):
                limit = 4 if core == way else 3
                if s <= limit:
                    yield way, lax.rem(source, 4) * 2 + core, source // 4 == c, s < limit

    def ring(s):
        for t in range(PIECES):
            for way, k, here, onward in ring_steps(s):

                @pl.when(here)
                def _(way=way, k=k, onward=onward, t=t):
                    copy = relay(k, way, piece(t), t)
                    copy.wait_recv()
                    if onward:
                        copy.start()

    loads[3].wait()
    r128 = column(128)
    r64 = r128 & 63
    ten = (r64 * 103) >> 10
    five = (r64 * 205) >> 10
    first_rows = (five & 1) * 288 + (ten + 6 * (r128 >> 6)) * 24 + r64 - 5 * five
    Sp[...] = dot(onehot(jnp.where(r64 < 60, first_rows, -1), OWN), E[0:OWN, :]).astype(BF)

    sk_lat = remote(Sp, E.at[864:992], sk_send.at[2], sk_recv.at[2], at(lat_prev, lon))
    sk_lat.start()

    ring(1)

    a = offs[0]
    shift_lat = jnp.where(a >= 6, a - 6, a)
    shift_lon = offs[1]
    n = column(WIN)
    valid, level, row, col = frame_cell(n)
    valid_t, _, row_t, _ = frame_cell(lax.broadcasted_iota(jnp.int32, (1, WIN), 1))
    source_col = col + shift_lon
    r = column(192)
    out_level = (r >= 96).astype(jnp.int32)
    frame_col = ((r - 96 * out_level) >> 3) - shift_lon
    left = frame_col < 0
    second = (frame_col >= 6).astype(jnp.int32)
    place = jnp.where(left, 160 + 6 + frame_col, HALF * second + frame_col - 6 * second)
    for b in range(3):
        frame_row = (r & 7) + (8 * b + 6) - shift_lat
        slot = (frame_row * 43) >> 8
        inner = 12 * (5 - (frame_row - 6 * slot)) + 6 * out_level
        Po[b] = onehot(240 * (slot - b) + inner + place, 720)

    ring(2)

    ring(3)

    sk_lon = [
        remote(E.at[0:144], E.at[576:720], sk_send.at[0], sk_recv.at[0], at(lat, lon_prev)),
        remote(E.at[288:432], E.at[720:864], sk_send.at[1], sk_recv.at[1], at(lat, lon_prev)),
    ]
    for copy in sk_lon:
        copy.start()

    w4x.wait_recv()
    w4r = remote(W4.at[128:192], W4.at[192:256], w4_send.at[2], w4_recv.at[2], sibling)
    w4r.start()
    wr = [
        remote(Wb.at[2, rows(j)], Wb.at[3, rows(j)], wr_send.at[j], wr_recv.at[j], sibling) for j in (0, 2, 1, 3)
    ]
    for arrived, onward in zip(wx, wr):
        arrived.wait_recv()
        onward.start()

    for w in range(4):
        source_row = row + (shift_lat + 6 * w)
        coarse_row = source_row >> 2
        coarse_col = source_col >> 2
        row_out = (coarse_row >= 6).astype(jnp.int32)
        col_out = (coarse_col >= 3).astype(jnp.int32)
        cell = 48 * col_out + row_out * (96 - 32 * col_out) + level + 6 * (coarse_row - 6 * row_out) + 2 * (coarse_col - 3 * col_out)
        Pl[w] = onehot(jnp.where(valid, cell, -1), 128)
        label = jnp.zeros((WIN, 1), jnp.int32)
        label_t = jnp.zeros((1, WIN), jnp.int32)
        for i in range(6):
            band = bands[lax.rem(lat * 24 + shift_lat + (6 * w + i), ROWS)]
            label = jnp.where(row == i, band, label)
            label_t = jnp.where(row_t == i, band, label_t)
        free = jnp.where(valid, 0, 1)
        seen = jnp.where(valid_t, 1, 0)
        match = jnp.where(label == label_t, 1, 0)
        bias[w] = jnp.where(seen * (match + free) > 0, 0.0, MASKED)

    sk_lat.wait_recv()
    sk_both = remote(E.at[864:928], E.at[992:1056], sk_send.at[3], sk_recv.at[3], at(lat, lon_prev))
    sk_both.start()

    @pl.when(is_home)
    def _():
        k = lax.rem(z, 4) * 2 + (1 - c)
        remote(xs, G.at[k], own_send.at[0], ring_recv.at[k, 0], sibling).wait_recv()

    loads[2].wait()
    ws.wait_recv()
    for copy in wr:
        copy.wait_recv()
    w4s.wait_recv()
    w4r.wait_recv()

    def term(k):
        return remote(msg.at[k], R.at[z], aa_send.at[k], aa_recv.at[z], at(lat, base + 8 * c + k))

    i64 = column(64)

    def level3(w):
        tails = G[pl.ds(4 * w, 4), 128:144, :].reshape(64, 512)
        for f in range(4):
            lanes = slice(512 * f, 512 * f + 512)
            Xt[0:128, lanes] = G[pl.ds(4 * w, 4), 32 * f : 32 * f + 32, :].reshape(128, 512)
            Xt[128:144, lanes] = dot(onehot((i16 >> 2) * 16 + 4 * f + (i16 & 3), 64), tails).astype(BF)
        PK[...] = dot_nt(Xt[...], Wb[...].reshape(768, D3)).astype(BF)
        terms = jnp.zeros((144, 512), F32)
        for h in range(4):
            q, k, v = (PK[:, 192 * h + 64 * i : 192 * h + 64 * i + 64] for i in range(3))
            terms = terms + dot(softmax_mix(q, k, v, None).astype(BF), W4[64 * h : 64 * h + 64, :])
        terms = terms.astype(BF)
        tails = jnp.zeros((64, 128), F32)
        for f in range(4):
            part = terms[:, 128 * f : 128 * f + 128]
            msg[pl.ds(4 * w, 4), 32 * f : 32 * f + 32, :] = part[0:128].reshape(4, 32, 128)
            tails = tails + dot(
                onehot(jnp.where(((i64 >> 2) & 3) == f, (i64 >> 4) * 4 + (i64 & 3), -1), 16), part[128:144]
            )
        msg[pl.ds(4 * w, 4), 128:144, :] = tails.astype(BF).reshape(4, 16, 128)
        for q in range(4):
            k = 4 * w + q

            @pl.when(base + 8 * c + k != lon)
            def _(k=k):
                term(k).start()

    flank = lax.rem(z, 4) // 2
    away = lax.rem(target + c, 2)
    nearer = flank + away * (1 - 2 * flank)
    level3(nearer)
    ring(4)
    level3(1 - nearer)

    @pl.when(is_home)
    def _():
        R[pl.ds(z, 1)] = msg[pl.ds(mine, 1)]

    for copy in sk_lon:
        copy.wait_recv()
    sk_both.wait_recv()
    for w in range(4):
        source_row = row + (shift_lat + 6 * w)
        cell = jnp.where(
            source_col < 12,
            288 * level + 24 * source_col + source_row,
            576 + 144 * level + 24 * (source_col - 12) + source_row,
        )
        third = (source_col >= 6).astype(jnp.int32) + (source_col >= 12).astype(jnp.int32)
        below = 864 + 64 * third + 10 * (source_col - 6 * third) + 5 * level + source_row - 24
        cell = jnp.where(source_row < 24, cell, below)
        width = 1056 if w == 3 else 864
        skF[w] = dot(onehot(jnp.where(valid, cell, -1), width), E[0:width, :]).astype(BF)

    total = jnp.zeros((144, 128), F32)
    for s in range(8):

        @pl.when(base + 2 * s + target != lon)
        def _(s=s):
            remote(msg.at[0], R.at[s], aa_send.at[0], aa_recv.at[s], sibling).wait_recv()

    for s in range(8):
        total = total + R[s].astype(F32)
    for f in range(4):
        lanes = slice(128 * f, 128 * f + 128)
        LE[0:32, lanes] = (cup[0:32, lanes] + total[32 * f : 32 * f + 32]).astype(BF)
        pick = jnp.where(
            (lax.broadcasted_iota(jnp.int32, (16, 16), 1) == 4 * f + i16) & (i16 < 4), 1.0, 0.0
        )
        rest = jnp.dot(pick, total[128:144], preferred_element_type=F32, precision=lax.Precision.HIGHEST)
        LE[32:48, lanes] = (cup[32:48, lanes] + rest).astype(BF)

    li_lon = remote(LE.at[0:48], LE.at[48:96], li_send.at[0], li_recv.at[0], at(lat, lon_prev))
    li_lat = remote(LE.at[0:16], LE.at[96:112], li_send.at[1], li_recv.at[1], at(lat_prev, lon))
    li_both = remote(LE.at[0:16], LE.at[112:128], li_send.at[2], li_recv.at[2], at(lat_prev, lon_prev))
    li = [li_both, li_lat, li_lon]
    for copy in li:
        copy.start()

    for load in loads[4:]:
        load.wait()

    def attend(w):
        reach = 128 if w == 3 else 96
        stream = skF[w].astype(F32) + dot(Pl[w, :, 0:reach], LE[0:reach, :])
        pk1[...] = dot(normalize(stream).astype(BF), w1v[...]).astype(BF)
        allowed = bias[w]
        for pair in range(4):
            both = []
            for h in (2 * pair, 2 * pair + 1):
                q, k, v = (pk1[:, 192 * h + 64 * i : 192 * h + 64 * i + 64] for i in range(3))
                both.append(softmax_mix(q, k, v, allowed))
            mix[:, 128 * pair : 128 * pair + 128] = jnp.concatenate(both, axis=1).astype(BF)
        AT[w] = stream + dot(mix[...], wo1v[...])

    def finish(parts):
        attended = jnp.concatenate([AT[w, first:last, :] for w, first, last in parts], axis=0)
        normed2 = normalize(attended).astype(BF)
        result = attended
        for f in range(2):
            hidden = jax.nn.gelu(dot(normed2, wiv[:, 1024 * f : 1024 * f + 1024])).astype(BF)
            result = result + dot(hidden, wfv[1024 * f : 1024 * f + 1024, :])
        result = result.astype(BF)
        at_row = 0
        for w, first, last in parts:
            Z[w + 1, first:last, :] = result[at_row : at_row + last - first]
            at_row += last - first

    def to_lon(w):
        return remote(
            Z.at[w + 1, HALF:WIN], Z.at[w + 1, WIN : WIN + HALF], lo_send.at[w], lo_recv.at[w], at(lat, lon_next)
        )

    to_lat = [
        remote(Z.at[4, 80:144], Z.at[0, 160:224], la_send.at[2], la_recv.at[2], at(lat_next, lon_next)),
        remote(Z.at[4, 80:144], Z.at[0, 80:144], la_send.at[1], la_recv.at[1], at(lat_next, lon)),
        remote(Z.at[4, 0:64], Z.at[0, 0:64], la_send.at[0], la_recv.at[0], at(lat_next, lon)),
    ]
    li_lon.wait_recv()
    attend(0)
    li_lat.wait_recv()
    li_both.wait_recv()
    attend(3)
    finish([(3, 0, WIN)])
    for copy in to_lat:
        copy.start()
    to_lon(3).start()
    attend(1)
    attend(2)
    finish([(w, HALF, WIN) for w in (0, 1, 2)])
    for w in (0, 1, 2):
        to_lon(w).start()
    finish([(w, 0, HALF) for w in (0, 1, 2)])
    for copy in to_lat:
        copy.wait_recv()
    for w in (3, 0, 1, 2):
        to_lon(w).wait_recv()
    for b in range(3):
        taken = dot(Po[b, :, 0:240], Z[b]) + dot(Po[b, :, 240:480], Z[b + 1]) + dot(Po[b, :, 480:720], Z[b + 2])
        out[:, 8 * b : 8 * b + 8, :] = taken.astype(BF).reshape(24, 8, D1)

    for copy in [*own, *wx, ws, w4x, w4s, w4r, *wr, sk_lat, *sk_lon, sk_both, *li, *to_lat]:
        copy.wait_send()

    @pl.when(jnp.logical_not(is_home))
    def _():
        own_sib.wait_send()

    for s in (1, 2, 3):
        for way, k, here, onward in ring_steps(s):
            if onward:

                @pl.when(here)
                def _(way=way, k=k):
                    relay(k, way, pl.ds(0, 144), 0).wait_send()

    for k in range(8):

        @pl.when(base + 8 * c + k != lon)
        def _(k=k):
            term(k).wait_send()

    for w in range(4):
        to_lon(w).wait_send()


def local(
    skip,
    coarse,
    offsets,
    bands,
    qkv3_weight,
    out3_weight,
    up_weight,
    qkv1_weight,
    out1_weight,
    mlp_in,
    mlp_out,
):
    cells = jnp.transpose(coarse, (1, 2, 0, 3)).reshape(CELLS3 // 2, 2, D3)
    vmem = pl.BlockSpec(memory_space=pltpu.VMEM)
    smem = pl.BlockSpec(memory_space=pltpu.SMEM)
    hbm = pl.BlockSpec(memory_space=ANY)
    dma = pltpu.SemaphoreType.DMA
    placed = pl.pallas_call(
        kernel,
        out_shape=jax.ShapeDtypeStruct((24, 24, D1), BF),
        in_specs=[smem, smem, vmem] + [hbm] * 8,
        out_specs=vmem,
        scratch_shapes=[
            pltpu.VMEM((144, 512), BF),
            pltpu.VMEM((8, 144, 512), BF),
            pltpu.VMEM((4, 192, D3), BF),
            pltpu.VMEM((64, D3), BF),
            pltpu.VMEM((D3, D1), BF),
            pltpu.VMEM((256, D1), BF),
            pltpu.VMEM((48, D1), F32),
            pltpu.VMEM((128, D1), BF),
            pltpu.VMEM((1056, D1), BF),
            pltpu.VMEM((4, WIN, D1), BF),
            pltpu.VMEM((4, WIN, WIN), F32),
            pltpu.VMEM((4, WIN, 128), BF),
            pltpu.VMEM((3, 192, 720), BF),
            pltpu.VMEM((144, D3), BF),
            pltpu.VMEM((144, 768), BF),
            pltpu.VMEM((8, 144, 128), BF),
            pltpu.VMEM((8, 144, 128), BF),
            pltpu.VMEM((128, D1), BF),
            pltpu.VMEM((D1, 3 * D1), BF),
            pltpu.VMEM((D1, D1), BF),
            pltpu.VMEM((D1, FF), BF),
            pltpu.VMEM((FF, D1), BF),
            pltpu.VMEM((WIN, 3 * D1), BF),
            pltpu.VMEM((WIN, D1), BF),
            pltpu.VMEM((4, WIN, D1), F32),
            pltpu.VMEM((5, 240, D1), BF),
            dma((8,)),
            dma((2 * PIECES + 1,)),
            dma((8, 2)),
            dma((8, PIECES)),
            dma((4,)),
            dma((4,)),
            dma((1,)),
            dma((1,)),
            dma((4,)),
            dma((4,)),
            dma((3,)),
            dma((3,)),
            dma((4,)),
            dma((4,)),
            dma((8,)),
            dma((8,)),
            dma((3,)),
            dma((3,)),
            dma((4,)),
            dma((4,)),
            dma((3,)),
            dma((3,)),
        ],
        compiler_params=pltpu.CompilerParams(
            collective_id=0, has_side_effects=True, vmem_limit_bytes=56 * 1024 * 1024
        ),
    )(
        offsets,
        bands,
        cells,
        jnp.transpose(skip, (0, 2, 1, 3)).reshape(OWN, D1),
        qkv3_weight.T,
        out3_weight,
        up_weight,
        qkv1_weight,
        out1_weight,
        mlp_in,
        mlp_out,
    )
    return jnp.transpose(placed.reshape(2, 12, 24, D1), (0, 2, 1, 3))


def solution(mesh):
    return jax.shard_map(
        local,
        mesh=mesh,
        in_specs=(
            P(None, "lat", "lon", None),
            P(None, "lat", "lon", None),
            P(),
            P(),
            P(None, "lon"),
            P("lon", None),
            P(),
            P(),
            P(),
            P(),
            P(),
        ),
        out_specs=P(None, "lat", "lon", None),
        check_vma=False,
    )
```

```python
import jax
import jax.numpy as jnp
from jax import lax
from jax.experimental import pallas as pl
from jax.experimental.pallas import tpu as pltpu
from jax.sharding import PartitionSpec as P

LATS = 8
LONS = 32
ROWS = 192
D3 = 2048
D1 = 512
FF = 2048
HEAD = 64
CELLS3 = 36
OWN = 576
PIECES = 3
PIECE = 144 // PIECES
SCALE = HEAD**-0.5
EPS = 1e-05
HALF = 80
WIN = 2 * HALF
MASKED = -1e30

F32 = jnp.float32
BF = jnp.bfloat16
MESH = pl.DeviceIdType.MESH
ANY = pl.ANY


def dot(a, b):
    return jnp.dot(a, b, preferred_element_type=F32)


def dot_nt(a, b):
    return lax.dot_general(a, b, (((1,), (1,)), ((), ())), preferred_element_type=F32)


def normalize(values):
    centred = values - jnp.mean(values, axis=-1, keepdims=True)
    spread = jnp.mean(centred * centred, axis=-1, keepdims=True)
    return centred * lax.rsqrt(spread + EPS)


def column(n):
    return lax.broadcasted_iota(jnp.int32, (n, 1), 0)


def onehot(target, width):
    n = target.shape[0]
    hit = lax.broadcasted_iota(jnp.int32, (n, width), 1) == target
    return jnp.where(hit, 1.0, 0.0).astype(BF)


def frame_cell(n):
    half = (n >= HALF).astype(jnp.int32)
    m = n - HALF * half
    valid = m < 72
    sixth = (m * 43) >> 8
    return valid, sixth & 1, 5 - (sixth >> 1), m - 6 * sixth + 6 * half


def softmax_mix(q, k, v, bias):
    scores = dot_nt(q, k) * SCALE
    if bias is not None:
        scores = scores + bias
    weights = jnp.exp(scores - jnp.max(scores, axis=1, keepdims=True))
    total = jnp.sum(weights, axis=1, keepdims=True)
    return dot(weights.astype(BF), v) * (1.0 / total)


def kernel(
    offs,
    bands,
    coarse,
    skip,
    wq,
    wo,
    up,
    w1,
    wo1,
    wi,
    wf,
    out,
    xs,
    G,
    Wb,
    wov,
    upv,
    W4,
    cup,
    Sp,
    E,
    skF,
    bias,
    Pl,
    Po,
    Xt,
    PK,
    msg,
    R,
    LE,
    w1v,
    w1p,
    wo1v,
    wiv,
    wfv,
    pk1,
    mix,
    AT,
    Z,
    loc,
    own_send,
    ring_send,
    ring_recv,
    wx_send,
    wx_recv,
    ws_send,
    ws_recv,
    wr_send,
    wr_recv,
    w4_send,
    w4_recv,
    sk_send,
    sk_recv,
    aa_send,
    aa_recv,
    li_send,
    li_recv,
    lo_send,
    lo_recv,
    la_send,
    la_recv,
):
    lat = lax.axis_index("lat")
    lon = lax.axis_index("lon")
    xl = lon // 16
    z = lax.rem(lon // 2, 8)
    c = lax.rem(lon, 2)
    base = xl * 16

    def at(lat_, lon_):
        return {"lat": lat_, "lon": lon_}

    def chip(z_, c_):
        return at(lat, base + 2 * lax.rem(z_ + 8, 8) + c_)

    sibling = at(lat, lon + 1 - 2 * c)
    across = lax.rem(lon + 16, 32)
    near = at(lat, across)
    far = at(lat + 1 - 2 * lax.rem(lat, 2), across)
    lon_next = lax.rem(lon + 1, LONS)
    lon_prev = lax.rem(lon + LONS - 1, LONS)
    lat_next = lax.rem(lat + 1, LATS)
    lat_prev = lax.rem(lat + LATS - 1, LATS)

    def remote(src, dst, send, recv, device):
        return pltpu.make_async_remote_copy(
            src_ref=src, dst_ref=dst, send_sem=send, recv_sem=recv, device_id=device, device_id_type=MESH
        )

    loads = [
        pltpu.make_async_copy(src, dst, loc.at[i])
        for i, (src, dst) in enumerate(
            [(up, upv), (wo, wov), (wq, Wb.at[0]), (skip, E.at[0:OWN]), (w1, w1v), (wo1, wo1v), (wi, wiv), (wf, wfv)]
        )
    ]
    for load in loads:
        load.start()

    barrier = pltpu.get_barrier_semaphore()
    greeted = [chip(z + d, c_) for d in range(1, 8) for c_ in (0, 1)] + [
        sibling,
        near,
        far,
        at(lat, lon_next),
        at(lat, lon_prev),
        at(lat_next, lon),
        at(lat_prev, lon),
        at(lat_next, lon_next),
        at(lat_prev, lon_prev),
    ]
    for device in greeted:
        pl.semaphore_signal(barrier, inc=1, device_id=device, device_id_type=MESH)

    cells = coarse[...].astype(F32).reshape(CELLS3, D3)
    cells = jnp.concatenate([cells, jnp.zeros((12, D3), F32)], axis=0)
    normed3 = normalize(cells).astype(BF)
    cells = cells.astype(BF)
    rest = jnp.zeros((16, 512), F32)
    i16 = column(16)
    for f in range(4):
        part = normed3[:, 512 * f : 512 * f + 512]
        xs[32 * f : 32 * f + 32, :] = part[0:32]
        pick = onehot(jnp.where((i16 >> 2) == f, i16 & 3, -1), 16)
        rest = rest + dot(pick, part[32:48])
    xs[128:144, :] = rest.astype(BF)

    for first in (64, 144, 224):
        Z[0, first : first + 16, :] = jnp.zeros((16, D1), BF)

    pl.semaphore_wait(barrier, len(greeted))

    target = z // 4
    mine = lax.rem(z, 4) * 2 + c
    is_home = target == c

    def piece(t):
        return pl.ds(PIECE * t, PIECE)

    own = [
        remote(
            xs.at[piece(t)],
            G.at[mine, piece(t)],
            own_send.at[2 * t + way],
            ring_recv.at[mine, t],
            chip(z + 1 - 2 * way, target),
        )
        for t in range(PIECES)
        for way in (0, 1)
    ]
    own_sib = remote(xs, G.at[mine], own_send.at[2 * PIECES], ring_recv.at[mine, 0], sibling)
    for copy in own:
        copy.start()

    @pl.when(jnp.logical_not(is_home))
    def _():
        own_sib.start()

    def rows(j):
        return pl.ds(48 * j, 48)

    wx = [
        remote(wq.at[rows(j)], Wb.at[2, rows(j)], wx_send.at[j], wx_recv.at[j], near if j < 2 else far)
        for j in (0, 2, 1, 3)
    ]
    for copy in wx:
        copy.start()
    ws = remote(wq, Wb.at[1], ws_send.at[0], ws_recv.at[0], sibling)
    ws.start()

    loads[0].wait()
    loads[1].wait()
    W4[0:64, :] = dot(wov[...], upv[...]).astype(BF)
    w4x = remote(W4.at[0:64], W4.at[128:192], w4_send.at[0], w4_recv.at[0], near)
    w4x.start()
    w4s = remote(W4.at[0:64], W4.at[64:128], w4_send.at[1], w4_recv.at[1], sibling)
    w4s.start()
    cup[...] = dot(cells, upv[...])

    @pl.when(is_home)
    def _():
        G[pl.ds(mine, 1)] = xs[...].reshape(1, 144, 512)

    def relay(k, way, rows_, t):
        block = G.at[k, rows_]
        return remote(block, block, ring_send.at[k, way], ring_recv.at[k, t], chip(z + 1 - 2 * way, c))

    def ring_steps(s):
        for way in (0, 1):
            source = lax.rem(z + (8 - s if way == 0 else s), 8)
            for core in (0, 1):
                limit = 4 if core == way else 3
                if s <= limit:
                    yield way, lax.rem(source, 4) * 2 + core, source // 4 == c, s < limit

    def ring(s):
        for t in range(PIECES):
            for way, k, here, onward in ring_steps(s):

                @pl.when(here)
                def _(way=way, k=k, onward=onward, t=t):
                    copy = relay(k, way, piece(t), t)
                    copy.wait_recv()
                    if onward:
                        copy.start()

    loads[3].wait()
    r128 = column(128)
    r64 = r128 & 63
    ten = (r64 * 103) >> 10
    five = (r64 * 205) >> 10
    first_rows = (five & 1) * 288 + (ten + 6 * (r128 >> 6)) * 24 + r64 - 5 * five
    Sp[...] = dot(onehot(jnp.where(r64 < 60, first_rows, -1), OWN), E[0:OWN, :]).astype(BF)

    sk_lat = remote(Sp, E.at[864:992], sk_send.at[2], sk_recv.at[2], at(lat_prev, lon))
    sk_lat.start()

    ring(1)

    loads[4].wait()
    for pair in range(4):
        for part in range(3):
            first = 384 * pair + 64 * part
            both = jnp.concatenate([w1v[:, first : first + 64], w1v[:, first + 192 : first + 256]], axis=1)
            if part == 0:
                both = (both.astype(F32) * SCALE).astype(BF)
            w1p[:, 512 * part + 128 * pair : 512 * part + 128 * pair + 128] = both

    ring(2)

    ring(3)

    sk_lon = [
        remote(E.at[0:144], E.at[576:720], sk_send.at[0], sk_recv.at[0], at(lat, lon_prev)),
        remote(E.at[288:432], E.at[720:864], sk_send.at[1], sk_recv.at[1], at(lat, lon_prev)),
    ]
    for copy in sk_lon:
        copy.start()

    w4x.wait_recv()
    w4r = remote(W4.at[128:192], W4.at[192:256], w4_send.at[2], w4_recv.at[2], sibling)
    w4r.start()
    wr = [
        remote(Wb.at[2, rows(j)], Wb.at[3, rows(j)], wr_send.at[j], wr_recv.at[j], sibling) for j in (0, 2, 1, 3)
    ]
    for arrived, onward in zip(wx, wr):
        arrived.wait_recv()
        onward.start()

    sk_lat.wait_recv()
    sk_both = remote(E.at[864:928], E.at[992:1056], sk_send.at[3], sk_recv.at[3], at(lat, lon_prev))
    sk_both.start()

    @pl.when(is_home)
    def _():
        k = lax.rem(z, 4) * 2 + (1 - c)
        remote(xs, G.at[k], own_send.at[0], ring_recv.at[k, 0], sibling).wait_recv()

    loads[2].wait()
    ws.wait_recv()
    for copy in wr:
        copy.wait_recv()
    w4s.wait_recv()
    w4r.wait_recv()

    def term(k):
        return remote(msg.at[k], R.at[z], aa_send.at[k], aa_recv.at[z], at(lat, base + 8 * c + k))

    i64 = column(64)

    def level3(w):
        tails = G[pl.ds(4 * w, 4), 128:144, :].reshape(64, 512)
        for f in range(4):
            lanes = slice(512 * f, 512 * f + 512)
            Xt[0:128, lanes] = G[pl.ds(4 * w, 4), 32 * f : 32 * f + 32, :].reshape(128, 512)
            Xt[128:144, lanes] = dot(onehot((i16 >> 2) * 16 + 4 * f + (i16 & 3), 64), tails).astype(BF)
        PK[...] = dot_nt(Xt[...], Wb[...].reshape(768, D3)).astype(BF)
        terms = jnp.zeros((144, 512), F32)
        for h in range(4):
            q, k, v = (PK[:, 192 * h + 64 * i : 192 * h + 64 * i + 64] for i in range(3))
            terms = terms + dot(softmax_mix(q, k, v, None).astype(BF), W4[64 * h : 64 * h + 64, :])
        terms = terms.astype(BF)
        tails = jnp.zeros((64, 128), F32)
        for f in range(4):
            part = terms[:, 128 * f : 128 * f + 128]
            msg[pl.ds(4 * w, 4), 32 * f : 32 * f + 32, :] = part[0:128].reshape(4, 32, 128)
            tails = tails + dot(
                onehot(jnp.where(((i64 >> 2) & 3) == f, (i64 >> 4) * 4 + (i64 & 3), -1), 16), part[128:144]
            )
        msg[pl.ds(4 * w, 4), 128:144, :] = tails.astype(BF).reshape(4, 16, 128)
        for q in range(4):
            k = 4 * w + q

            @pl.when(base + 8 * c + k != lon)
            def _(k=k):
                term(k).start()

    flank = lax.rem(z, 4) // 2
    away = lax.rem(target + c, 2)
    nearer = flank + away * (1 - 2 * flank)
    level3(nearer)
    ring(4)
    level3(1 - nearer)

    @pl.when(is_home)
    def _():
        R[pl.ds(z, 1)] = msg[pl.ds(mine, 1)]

    a = offs[0]
    shift_lat = jnp.where(a >= 6, a - 6, a)
    shift_lon = offs[1]
    n = column(WIN)
    valid, level, row, col = frame_cell(n)
    valid_t, _, row_t, _ = frame_cell(lax.broadcasted_iota(jnp.int32, (1, WIN), 1))
    source_col = col + shift_lon
    for w in range(4):
        source_row = row + (shift_lat + 6 * w)
        coarse_row = source_row >> 2
        coarse_col = source_col >> 2
        row_out = (coarse_row >= 6).astype(jnp.int32)
        col_out = (coarse_col >= 3).astype(jnp.int32)
        cell = 48 * col_out + row_out * (96 - 32 * col_out) + level + 6 * (coarse_row - 6 * row_out) + 2 * (coarse_col - 3 * col_out)
        Pl[w] = onehot(jnp.where(valid, cell, -1), 128)
        label = jnp.zeros((WIN, 1), jnp.int32)
        label_t = jnp.zeros((1, WIN), jnp.int32)
        for i in range(6):
            band = bands[lax.rem(lat * 24 + shift_lat + (6 * w + i), ROWS)]
            label = jnp.where(row == i, band, label)
            label_t = jnp.where(row_t == i, band, label_t)
        free = jnp.where(valid, 0, 1)
        seen = jnp.where(valid_t, 1, 0)
        match = jnp.where(label == label_t, 1, 0)
        bias[w] = jnp.where(seen * (match + free) > 0, 0.0, MASKED)

    r = column(192)
    out_level = (r >= 96).astype(jnp.int32)
    frame_col = ((r - 96 * out_level) >> 3) - shift_lon
    left = frame_col < 0
    second = (frame_col >= 6).astype(jnp.int32)
    place = jnp.where(left, 160 + 6 + frame_col, HALF * second + frame_col - 6 * second)
    for b in range(3):
        frame_row = (r & 7) + (8 * b + 6) - shift_lat
        slot = (frame_row * 43) >> 8
        inner = 12 * (5 - (frame_row - 6 * slot)) + 6 * out_level
        Po[b] = onehot(240 * (slot - b) + inner + place, 720)

    for copy in sk_lon:
        copy.wait_recv()
    sk_both.wait_recv()
    for w in range(4):
        source_row = row + (shift_lat + 6 * w)
        cell = jnp.where(
            source_col < 12,
            288 * level + 24 * source_col + source_row,
            576 + 144 * level + 24 * (source_col - 12) + source_row,
        )
        third = (source_col >= 6).astype(jnp.int32) + (source_col >= 12).astype(jnp.int32)
        below = 864 + 64 * third + 10 * (source_col - 6 * third) + 5 * level + source_row - 24
        cell = jnp.where(source_row < 24, cell, below)
        width = 1056 if w == 3 else 864
        skF[w] = dot(onehot(jnp.where(valid, cell, -1), width), E[0:width, :]).astype(BF)

    total = jnp.zeros((144, 128), F32)
    for s in range(8):

        @pl.when(base + 2 * s + target != lon)
        def _(s=s):
            remote(msg.at[0], R.at[s], aa_send.at[0], aa_recv.at[s], sibling).wait_recv()

    for s in range(8):
        total = total + R[s].astype(F32)
    for f in range(4):
        lanes = slice(128 * f, 128 * f + 128)
        LE[0:32, lanes] = (cup[0:32, lanes] + total[32 * f : 32 * f + 32]).astype(BF)
        pick = jnp.where(
            (lax.broadcasted_iota(jnp.int32, (16, 16), 1) == 4 * f + i16) & (i16 < 4), 1.0, 0.0
        )
        rest = jnp.dot(pick, total[128:144], preferred_element_type=F32, precision=lax.Precision.HIGHEST)
        LE[32:48, lanes] = (cup[32:48, lanes] + rest).astype(BF)

    li_lon = remote(LE.at[0:48], LE.at[48:96], li_send.at[0], li_recv.at[0], at(lat, lon_prev))
    li_lat = remote(LE.at[0:16], LE.at[96:112], li_send.at[1], li_recv.at[1], at(lat_prev, lon))
    li_both = remote(LE.at[0:16], LE.at[112:128], li_send.at[2], li_recv.at[2], at(lat_prev, lon_prev))
    li = [li_both, li_lat, li_lon]
    for copy in li:
        copy.start()

    for load in loads[5:]:
        load.wait()

    low = lax.broadcasted_iota(jnp.int32, (WIN, 128), 1) < HEAD
    zero = jnp.zeros((WIN, 128), BF)
    one = jnp.ones((WIN, 128), BF)

    def attend(w):
        reach = 128 if w == 3 else 96
        stream = skF[w].astype(F32) + dot(Pl[w, :, 0:reach], LE[0:reach, :])
        pk1[...] = dot(normalize(stream).astype(BF), w1p[...]).astype(BF)
        allowed = bias[w]
        for pair in range(4):
            lanes = slice(128 * pair, 128 * pair + 128)
            q, k, v = (pk1[:, 512 * i + 128 * pair : 512 * i + 128 * pair + 128] for i in range(3))
            sums = []
            for first in (True, False):
                here = low if first else jnp.logical_not(low)
                scores = dot_nt(jnp.where(here, q, zero), k) + allowed
                weights = jnp.exp(scores - jnp.max(scores, axis=1, keepdims=True)).astype(BF)
                sums.append(dot(weights, jnp.where(here, v, one)))
            mixed = jnp.where(low, sums[0], sums[1])
            total = pltpu.roll(jnp.where(low, sums[1], sums[0]), 64, 1)
            mix[:, lanes] = (mixed * (1.0 / total)).astype(BF)
        AT[w] = stream + dot(mix[...], wo1v[...])

    def finish(parts):
        attended = jnp.concatenate([AT[w, first:last, :] for w, first, last in parts], axis=0)
        normed2 = normalize(attended).astype(BF)
        result = attended
        for f in range(2):
            hidden = jax.nn.gelu(dot(normed2, wiv[:, 1024 * f : 1024 * f + 1024])).astype(BF)
            result = result + dot(hidden, wfv[1024 * f : 1024 * f + 1024, :])
        result = result.astype(BF)
        at_row = 0
        for w, first, last in parts:
            Z[w + 1, first:last, :] = result[at_row : at_row + last - first]
            at_row += last - first

    def to_lon(w):
        return remote(
            Z.at[w + 1, HALF:WIN], Z.at[w + 1, WIN : WIN + HALF], lo_send.at[w], lo_recv.at[w], at(lat, lon_next)
        )

    to_lat = [
        remote(Z.at[4, 80:144], Z.at[0, 160:224], la_send.at[2], la_recv.at[2], at(lat_next, lon_next)),
        remote(Z.at[4, 80:144], Z.at[0, 80:144], la_send.at[1], la_recv.at[1], at(lat_next, lon)),
        remote(Z.at[4, 0:64], Z.at[0, 0:64], la_send.at[0], la_recv.at[0], at(lat_next, lon)),
    ]
    li_lon.wait_recv()
    attend(0)
    li_lat.wait_recv()
    li_both.wait_recv()
    attend(3)
    finish([(3, 0, WIN), (0, HALF, WIN)])
    for copy in to_lat:
        copy.start()
    to_lon(3).start()
    to_lon(0).start()
    attend(1)
    attend(2)
    finish([(1, HALF, WIN), (2, HALF, WIN)])
    to_lon(1).start()
    to_lon(2).start()
    finish([(w, 0, HALF) for w in (0, 1, 2)])
    for copy in to_lat:
        copy.wait_recv()
    for w in (3, 0, 1, 2):
        to_lon(w).wait_recv()
    for b in range(3):
        taken = dot(Po[b, :, 0:240], Z[b]) + dot(Po[b, :, 240:480], Z[b + 1]) + dot(Po[b, :, 480:720], Z[b + 2])
        out[:, 8 * b : 8 * b + 8, :] = taken.astype(BF).reshape(24, 8, D1)

    for copy in [*own, *wx, ws, w4x, w4s, w4r, *wr, sk_lat, *sk_lon, sk_both, *li, *to_lat]:
        copy.wait_send()

    @pl.when(jnp.logical_not(is_home))
    def _():
        own_sib.wait_send()

    for s in (1, 2, 3):
        for way, k, here, onward in ring_steps(s):
            if onward:

                @pl.when(here)
                def _(way=way, k=k):
                    relay(k, way, pl.ds(0, 144), 0).wait_send()

    for k in range(8):

        @pl.when(base + 8 * c + k != lon)
        def _(k=k):
            term(k).wait_send()

    for w in range(4):
        to_lon(w).wait_send()


def local(
    skip,
    coarse,
    offsets,
    bands,
    qkv3_weight,
    out3_weight,
    up_weight,
    qkv1_weight,
    out1_weight,
    mlp_in,
    mlp_out,
):
    cells = jnp.transpose(coarse, (1, 2, 0, 3)).reshape(CELLS3 // 2, 2, D3)
    vmem = pl.BlockSpec(memory_space=pltpu.VMEM)
    smem = pl.BlockSpec(memory_space=pltpu.SMEM)
    hbm = pl.BlockSpec(memory_space=ANY)
    dma = pltpu.SemaphoreType.DMA
    placed = pl.pallas_call(
        kernel,
        out_shape=jax.ShapeDtypeStruct((24, 24, D1), BF),
        in_specs=[smem, smem, vmem] + [hbm] * 8,
        out_specs=vmem,
        scratch_shapes=[
            pltpu.VMEM((144, 512), BF),
            pltpu.VMEM((8, 144, 512), BF),
            pltpu.VMEM((4, 192, D3), BF),
            pltpu.VMEM((64, D3), BF),
            pltpu.VMEM((D3, D1), BF),
            pltpu.VMEM((256, D1), BF),
            pltpu.VMEM((48, D1), F32),
            pltpu.VMEM((128, D1), BF),
            pltpu.VMEM((1056, D1), BF),
            pltpu.VMEM((4, WIN, D1), BF),
            pltpu.VMEM((4, WIN, WIN), F32),
            pltpu.VMEM((4, WIN, 128), BF),
            pltpu.VMEM((3, 192, 720), BF),
            pltpu.VMEM((144, D3), BF),
            pltpu.VMEM((144, 768), BF),
            pltpu.VMEM((8, 144, 128), BF),
            pltpu.VMEM((8, 144, 128), BF),
            pltpu.VMEM((128, D1), BF),
            pltpu.VMEM((D1, 3 * D1), BF),
            pltpu.VMEM((D1, 3 * D1), BF),
            pltpu.VMEM((D1, D1), BF),
            pltpu.VMEM((D1, FF), BF),
            pltpu.VMEM((FF, D1), BF),
            pltpu.VMEM((WIN, 3 * D1), BF),
            pltpu.VMEM((WIN, D1), BF),
            pltpu.VMEM((4, WIN, D1), F32),
            pltpu.VMEM((5, 240, D1), BF),
            dma((8,)),
            dma((2 * PIECES + 1,)),
            dma((8, 2)),
            dma((8, PIECES)),
            dma((4,)),
            dma((4,)),
            dma((1,)),
            dma((1,)),
            dma((4,)),
            dma((4,)),
            dma((3,)),
            dma((3,)),
            dma((4,)),
            dma((4,)),
            dma((8,)),
            dma((8,)),
            dma((3,)),
            dma((3,)),
            dma((4,)),
            dma((4,)),
            dma((3,)),
            dma((3,)),
        ],
        compiler_params=pltpu.CompilerParams(
            collective_id=0, has_side_effects=True, vmem_limit_bytes=56 * 1024 * 1024
        ),
    )(
        offsets,
        bands,
        cells,
        jnp.transpose(skip, (0, 2, 1, 3)).reshape(OWN, D1),
        qkv3_weight.T,
        out3_weight,
        up_weight,
        qkv1_weight,
        out1_weight,
        mlp_in,
        mlp_out,
    )
    return jnp.transpose(placed.reshape(2, 12, 24, D1), (0, 2, 1, 3))


def solution(mesh):
    return jax.shard_map(
        local,
        mesh=mesh,
        in_specs=(
            P(None, "lat", "lon", None),
            P(None, "lat", "lon", None),
            P(),
            P(),
            P(None, "lon"),
            P("lon", None),
            P(),
            P(),
            P(),
            P(),
            P(),
        ),
        out_specs=P(None, "lat", "lon", None),
        check_vma=False,
    )
```

```python
import jax
import jax.numpy as jnp
from jax import lax
from jax.experimental import pallas as pl
from jax.experimental.pallas import tpu as pltpu
from jax.sharding import PartitionSpec as P

LATS = 8
LONS = 32
ROWS = 192
D3 = 2048
D1 = 512
FF = 2048
HEAD = 64
CELLS3 = 36
OWN = 576
PIECES = 3
PIECE = 144 // PIECES
SCALE = HEAD**-0.5
EPS = 1e-05
HALF = 80
WIN = 2 * HALF
MASKED = -1e30

F32 = jnp.float32
BF = jnp.bfloat16
MESH = pl.DeviceIdType.MESH
ANY = pl.ANY


def dot(a, b):
    return jnp.dot(a, b, preferred_element_type=F32)


def dot_nt(a, b):
    return lax.dot_general(a, b, (((1,), (1,)), ((), ())), preferred_element_type=F32)


def normalize(values):
    centred = values - jnp.mean(values, axis=-1, keepdims=True)
    spread = jnp.mean(centred * centred, axis=-1, keepdims=True)
    return centred * lax.rsqrt(spread + EPS)


def column(n):
    return lax.broadcasted_iota(jnp.int32, (n, 1), 0)


def onehot(target, width):
    n = target.shape[0]
    hit = lax.broadcasted_iota(jnp.int32, (n, width), 1) == target
    return jnp.where(hit, 1.0, 0.0).astype(BF)


def frame_cell(n):
    half = (n >= HALF).astype(jnp.int32)
    m = n - HALF * half
    valid = m < 72
    sixth = (m * 43) >> 8
    return valid, sixth & 1, 5 - (sixth >> 1), m - 6 * sixth + 6 * half


def pair_mix(q, k, v, allowed):
    low = lax.broadcasted_iota(jnp.int32, q.shape, 1) < HEAD
    sums = []
    for here in (low, jnp.logical_not(low)):
        scores = dot_nt(jnp.where(here, q, jnp.zeros_like(q)), k)
        if allowed is not None:
            scores = scores + allowed
        weights = jnp.exp(scores - jnp.max(scores, axis=1, keepdims=True)).astype(BF)
        sums.append(dot(weights, jnp.where(here, v, jnp.ones_like(v))))
    total = pltpu.roll(jnp.where(low, sums[1], sums[0]), HEAD, 1)
    return jnp.where(low, sums[0], sums[1]) * (1.0 / total)


def kernel(
    offs,
    bands,
    coarse,
    skip,
    wq,
    wo,
    up,
    w1,
    wo1,
    wi,
    wf,
    out,
    xs,
    G,
    Wb,
    wov,
    upv,
    W4,
    cup,
    Sp,
    E,
    skF,
    bias,
    Pl,
    PA,
    PB,
    PC,
    OA,
    Xt,
    PK,
    msg,
    R,
    LE,
    w1v,
    w1p,
    wo1v,
    wiv,
    wfv,
    pk1,
    mix,
    AT,
    Z,
    ZB,
    loc,
    own_send,
    ring_send,
    ring_recv,
    wx_send,
    wx_recv,
    ws_send,
    ws_recv,
    wr_send,
    wr_recv,
    w4_send,
    w4_recv,
    sk_send,
    sk_recv,
    aa_send,
    aa_recv,
    li_send,
    li_recv,
    lo_send,
    lo_recv,
    la_send,
    la_recv,
):
    lat = lax.axis_index("lat")
    lon = lax.axis_index("lon")
    xl = lon // 16
    z = lax.rem(lon // 2, 8)
    c = lax.rem(lon, 2)
    base = xl * 16

    def at(lat_, lon_):
        return {"lat": lat_, "lon": lon_}

    def chip(z_, c_):
        return at(lat, base + 2 * lax.rem(z_ + 8, 8) + c_)

    sibling = at(lat, lon + 1 - 2 * c)
    across = lax.rem(lon + 16, 32)
    near = at(lat, across)
    far = at(lat + 1 - 2 * lax.rem(lat, 2), across)
    lon_next = lax.rem(lon + 1, LONS)
    lon_prev = lax.rem(lon + LONS - 1, LONS)
    lat_next = lax.rem(lat + 1, LATS)
    lat_prev = lax.rem(lat + LATS - 1, LATS)

    def remote(src, dst, send, recv, device):
        return pltpu.make_async_remote_copy(
            src_ref=src, dst_ref=dst, send_sem=send, recv_sem=recv, device_id=device, device_id_type=MESH
        )

    loads = [
        pltpu.make_async_copy(src, dst, loc.at[i])
        for i, (src, dst) in enumerate(
            [(up, upv), (wo, wov), (wq, Wb.at[:, 0]), (skip, E.at[0:OWN]), (w1, w1v), (wo1, wo1v), (wi, wiv), (wf, wfv)]
        )
    ]
    for load in loads:
        load.start()

    barrier = pltpu.get_barrier_semaphore()
    greeted = [chip(z + d, c_) for d in range(1, 8) for c_ in (0, 1)] + [
        sibling,
        near,
        far,
        at(lat, lon_next),
        at(lat, lon_prev),
        at(lat_next, lon),
        at(lat_prev, lon),
        at(lat_next, lon_next),
        at(lat_prev, lon_prev),
    ]
    for device in greeted:
        pl.semaphore_signal(barrier, inc=1, device_id=device, device_id_type=MESH)

    cells = coarse[...].astype(F32).reshape(CELLS3, D3)
    cells = jnp.concatenate([cells, jnp.zeros((12, D3), F32)], axis=0)
    normed3 = normalize(cells).astype(BF)
    cells = cells.astype(BF)
    rest = jnp.zeros((16, 512), F32)
    i16 = column(16)
    for f in range(4):
        part = normed3[:, 512 * f : 512 * f + 512]
        xs[32 * f : 32 * f + 32, :] = part[0:32]
        pick = onehot(jnp.where((i16 >> 2) == f, i16 & 3, -1), 16)
        rest = rest + dot(pick, part[32:48])
    xs[128:144, :] = rest.astype(BF)

    for first in (64, 144):
        Z[0, first : first + 16, :] = jnp.zeros((16, D1), BF)
    ZB[0, 64:80, :] = jnp.zeros((16, D1), BF)

    pl.semaphore_wait(barrier, len(greeted))

    target = z // 4
    mine = lax.rem(z, 4) * 2 + c
    is_home = target == c

    def piece(t):
        return pl.ds(PIECE * t, PIECE)

    own = [
        remote(
            xs.at[piece(t)],
            G.at[mine, piece(t)],
            own_send.at[2 * t + way],
            ring_recv.at[mine, t],
            chip(z + 1 - 2 * way, target),
        )
        for t in range(PIECES)
        for way in (0, 1)
    ]
    own_sib = remote(xs, G.at[mine], own_send.at[2 * PIECES], ring_recv.at[mine, 0], sibling)
    for copy in own:
        copy.start()

    @pl.when(jnp.logical_not(is_home))
    def _():
        own_sib.start()

    def rows(j):
        return pl.ds(16 * j, 16)

    wx = [
        remote(wq.at[:, rows(j)], Wb.at[:, 2, rows(j)], wx_send.at[j], wx_recv.at[j], near if j < 2 else far)
        for j in (0, 2, 1, 3)
    ]
    for copy in wx:
        copy.start()
    ws = remote(wq, Wb.at[:, 1], ws_send.at[0], ws_recv.at[0], sibling)
    ws.start()

    loads[0].wait()
    loads[1].wait()
    W4[0:64, :] = dot(wov[...], upv[...]).astype(BF)
    w4x = remote(W4.at[0:64], W4.at[128:192], w4_send.at[0], w4_recv.at[0], near)
    w4x.start()
    w4s = remote(W4.at[0:64], W4.at[64:128], w4_send.at[1], w4_recv.at[1], sibling)
    w4s.start()
    cup[...] = dot(cells, upv[...])

    @pl.when(is_home)
    def _():
        G[pl.ds(mine, 1)] = xs[...].reshape(1, 144, 512)

    def relay(k, way, rows_, t):
        block = G.at[k, rows_]
        return remote(block, block, ring_send.at[k, way], ring_recv.at[k, t], chip(z + 1 - 2 * way, c))

    def ring_steps(s):
        for way in (0, 1):
            source = lax.rem(z + (8 - s if way == 0 else s), 8)
            for core in (0, 1):
                limit = 4 if core == way else 3
                if s <= limit:
                    yield way, lax.rem(source, 4) * 2 + core, source // 4 == c, s < limit

    def ring(s):
        for t in range(PIECES):
            for way, k, here, onward in ring_steps(s):

                @pl.when(here)
                def _(way=way, k=k, onward=onward, t=t):
                    copy = relay(k, way, piece(t), t)
                    copy.wait_recv()
                    if onward:
                        copy.start()

    loads[3].wait()
    r128 = column(128)
    r64 = r128 & 63
    ten = (r64 * 103) >> 10
    five = (r64 * 205) >> 10
    first_rows = (five & 1) * 288 + (ten + 6 * (r128 >> 6)) * 24 + r64 - 5 * five
    Sp[...] = dot(onehot(jnp.where(r64 < 60, first_rows, -1), OWN), E[0:OWN, :]).astype(BF)

    sk_lat = remote(Sp, E.at[864:992], sk_send.at[2], sk_recv.at[2], at(lat_prev, lon))
    sk_lat.start()

    ring(1)

    ring(2)

    ring(3)

    sk_lon = [
        remote(E.at[0:144], E.at[576:720], sk_send.at[0], sk_recv.at[0], at(lat, lon_prev)),
        remote(E.at[288:432], E.at[720:864], sk_send.at[1], sk_recv.at[1], at(lat, lon_prev)),
    ]
    for copy in sk_lon:
        copy.start()

    loads[4].wait()
    for pair in range(4):
        for part in range(3):
            first = 384 * pair + 64 * part
            both = jnp.concatenate([w1v[:, first : first + 64], w1v[:, first + 192 : first + 256]], axis=1)
            if part == 0:
                both = (both.astype(F32) * SCALE).astype(BF)
            w1p[:, 512 * part + 128 * pair : 512 * part + 128 * pair + 128] = both

    w4x.wait_recv()
    w4r = remote(W4.at[128:192], W4.at[192:256], w4_send.at[2], w4_recv.at[2], sibling)
    w4r.start()
    wr = [
        remote(Wb.at[:, 2, rows(j)], Wb.at[:, 3, rows(j)], wr_send.at[j], wr_recv.at[j], sibling) for j in (0, 2, 1, 3)
    ]
    for arrived, onward in zip(wx, wr):
        arrived.wait_recv()
        onward.start()

    sk_lat.wait_recv()
    sk_both = remote(E.at[864:928], E.at[992:1056], sk_send.at[3], sk_recv.at[3], at(lat, lon_prev))
    sk_both.start()

    @pl.when(is_home)
    def _():
        k = lax.rem(z, 4) * 2 + (1 - c)
        remote(xs, G.at[k], own_send.at[0], ring_recv.at[k, 0], sibling).wait_recv()

    loads[2].wait()
    ws.wait_recv()
    for copy in wr:
        copy.wait_recv()
    w4s.wait_recv()
    w4r.wait_recv()

    def term(k):
        return remote(msg.at[k], R.at[z], aa_send.at[k], aa_recv.at[z], at(lat, base + 8 * c + k))

    i64 = column(64)

    def level3(w):
        tails = G[pl.ds(4 * w, 4), 128:144, :].reshape(64, 512)
        for f in range(4):
            lanes = slice(512 * f, 512 * f + 512)
            Xt[0:128, lanes] = G[pl.ds(4 * w, 4), 32 * f : 32 * f + 32, :].reshape(128, 512)
            Xt[128:144, lanes] = dot(onehot((i16 >> 2) * 16 + 4 * f + (i16 & 3), 64), tails).astype(BF)
        packed = dot_nt(Xt[...], Wb[...].reshape(768, D3))
        PK[:, 0:256] = (packed[:, 0:256] * SCALE).astype(BF)
        PK[:, 256:768] = packed[:, 256:768].astype(BF)
        terms = jnp.zeros((144, 512), F32)
        for pair in range(2):
            q, k, v = (PK[:, 256 * i + 128 * pair : 256 * i + 128 * pair + 128] for i in range(3))
            terms = terms + dot(pair_mix(q, k, v, None).astype(BF), W4[128 * pair : 128 * pair + 128, :])
        terms = terms.astype(BF)
        tails = jnp.zeros((64, 128), F32)
        for f in range(4):
            part = terms[:, 128 * f : 128 * f + 128]
            msg[pl.ds(4 * w, 4), 32 * f : 32 * f + 32, :] = part[0:128].reshape(4, 32, 128)
            tails = tails + dot(
                onehot(jnp.where(((i64 >> 2) & 3) == f, (i64 >> 4) * 4 + (i64 & 3), -1), 16), part[128:144]
            )
        msg[pl.ds(4 * w, 4), 128:144, :] = tails.astype(BF).reshape(4, 16, 128)
        for q in range(4):
            k = 4 * w + q

            @pl.when(base + 8 * c + k != lon)
            def _(k=k):
                term(k).start()

    flank = lax.rem(z, 4) // 2
    away = lax.rem(target + c, 2)
    nearer = flank + away * (1 - 2 * flank)
    level3(nearer)
    ring(4)
    level3(1 - nearer)

    @pl.when(is_home)
    def _():
        R[pl.ds(z, 1)] = msg[pl.ds(mine, 1)]

    a = offs[0]
    shift_lat = jnp.where(a >= 6, a - 6, a)
    shift_lon = offs[1]
    n = column(WIN)
    valid, level, row, col = frame_cell(n)
    valid_t, _, row_t, _ = frame_cell(lax.broadcasted_iota(jnp.int32, (1, WIN), 1))
    source_col = col + shift_lon
    for w in range(4):
        source_row = row + (shift_lat + 6 * w)
        coarse_row = source_row >> 2
        coarse_col = source_col >> 2
        row_out = (coarse_row >= 6).astype(jnp.int32)
        col_out = (coarse_col >= 3).astype(jnp.int32)
        cell = 48 * col_out + row_out * (96 - 32 * col_out) + level + 6 * (coarse_row - 6 * row_out) + 2 * (coarse_col - 3 * col_out)
        Pl[w] = onehot(jnp.where(valid, cell, -1), 128)
        label = jnp.zeros((WIN, 1), jnp.int32)
        label_t = jnp.zeros((1, WIN), jnp.int32)
        for i in range(6):
            band = bands[lax.rem(lat * 24 + shift_lat + (6 * w + i), ROWS)]
            label = jnp.where(row == i, band, label)
            label_t = jnp.where(row_t == i, band, label_t)
        free = jnp.where(valid, 0, 1)
        seen = jnp.where(valid_t, 1, 0)
        match = jnp.where(label == label_t, 1, 0)
        bias[w] = jnp.where(seen * (match + free) > 0, 0.0, MASKED)

    r = column(192)
    out_level = (r >= 96).astype(jnp.int32)
    frame_col = ((r - 96 * out_level) >> 3) - shift_lon
    left = frame_col < 0
    second = (frame_col >= 6).astype(jnp.int32)
    for b in range(3):
        frame_row = (r & 7) + (8 * b + 6) - shift_lat
        slot = (frame_row * 43) >> 8
        inner = 12 * (5 - (frame_row - 6 * slot)) + 6 * out_level + frame_col
        kept = WIN * (slot - max(b, 1)) + (HALF - 6) * second + inner
        PA[b] = onehot(jnp.where(left, -1, kept), 3 * WIN)
        PB[b] = onehot(jnp.where(left, HALF * (slot - b) + inner + 6, -1), 3 * HALF)
        if b == 0:
            PC[...] = onehot(jnp.where(left | (slot > 0), -1, kept + WIN), WIN)

    for copy in sk_lon:
        copy.wait_recv()
    sk_both.wait_recv()
    for w in range(4):
        source_row = row + (shift_lat + 6 * w)
        cell = jnp.where(
            source_col < 12,
            288 * level + 24 * source_col + source_row,
            576 + 144 * level + 24 * (source_col - 12) + source_row,
        )
        third = (source_col >= 6).astype(jnp.int32) + (source_col >= 12).astype(jnp.int32)
        below = 864 + 64 * third + 10 * (source_col - 6 * third) + 5 * level + source_row - 24
        cell = jnp.where(source_row < 24, cell, below)
        width = 1056 if w == 3 else 864
        skF[w] = dot(onehot(jnp.where(valid, cell, -1), width), E[0:width, :]).astype(BF)

    total = jnp.zeros((144, 128), F32)
    for s in range(8):

        @pl.when(base + 2 * s + target != lon)
        def _(s=s):
            remote(msg.at[0], R.at[s], aa_send.at[0], aa_recv.at[s], sibling).wait_recv()

    for s in range(8):
        total = total + R[s].astype(F32)
    for f in range(4):
        lanes = slice(128 * f, 128 * f + 128)
        LE[0:32, lanes] = (cup[0:32, lanes] + total[32 * f : 32 * f + 32]).astype(BF)
        rest = jnp.concatenate([total[128 + 4 * f : 132 + 4 * f], jnp.zeros((12, 128), F32)], axis=0)
        LE[32:48, lanes] = (cup[32:48, lanes] + rest).astype(BF)

    li_lon = remote(LE.at[0:48], LE.at[48:96], li_send.at[0], li_recv.at[0], at(lat, lon_prev))
    li_lat = remote(LE.at[0:16], LE.at[96:112], li_send.at[1], li_recv.at[1], at(lat_prev, lon))
    li_both = remote(LE.at[0:16], LE.at[112:128], li_send.at[2], li_recv.at[2], at(lat_prev, lon_prev))
    li = [li_both, li_lat, li_lon]
    for copy in li:
        copy.start()

    for load in loads[5:]:
        load.wait()

    def project(parts, reach):
        chosen = jnp.concatenate([Pl[w, first:last, 0:reach] for w, first, last in parts], axis=0)
        taken = jnp.concatenate([skF[w, first:last, :] for w, first, last in parts], axis=0)
        stream = taken.astype(F32) + dot(chosen, LE[0:reach, :])
        packed = dot(normalize(stream).astype(BF), w1p[...]).astype(BF)
        at_row = 0
        for w, first, last in parts:
            here = slice(at_row, at_row + last - first)
            AT[w, first:last, :] = stream[here]
            pk1[w, first:last, :] = packed[here]
            at_row += last - first

    def attend(w):
        for pair in range(4):
            lanes = slice(128 * pair, 128 * pair + 128)
            q, k, v = (pk1[w, :, 512 * i + 128 * pair : 512 * i + 128 * pair + 128] for i in range(3))
            mix[:, lanes] = pair_mix(q, k, v, bias[w]).astype(BF)
        AT[w] = AT[w] + dot(mix[...], wo1v[...])

    def finish(parts):
        attended = jnp.concatenate([AT[w, first:last, :] for w, first, last in parts], axis=0)
        normed2 = normalize(attended).astype(BF)
        result = attended
        for f in range(2):
            hidden = jax.nn.gelu(dot(normed2, wiv[:, 1024 * f : 1024 * f + 1024])).astype(BF)
            result = result + dot(hidden, wfv[1024 * f : 1024 * f + 1024, :])
        result = result.astype(BF)
        at_row = 0
        for w, first, last in parts:
            Z[w + 1, first:last, :] = result[at_row : at_row + last - first]
            at_row += last - first

    def to_lon(w):
        return remote(
            Z.at[w + 1, HALF:WIN], ZB.at[w + 1], lo_send.at[w], lo_recv.at[w], at(lat, lon_next)
        )

    to_lat = [
        remote(Z.at[4, 80:144], ZB.at[0, 0:64], la_send.at[2], la_recv.at[2], at(lat_next, lon_next)),
        remote(Z.at[4, 80:144], Z.at[0, 80:144], la_send.at[1], la_recv.at[1], at(lat_next, lon)),
        remote(Z.at[4, 0:64], Z.at[0, 0:64], la_send.at[0], la_recv.at[0], at(lat_next, lon)),
    ]
    project([(w, 0, HALF) for w in (0, 1, 2)], 48)
    li_lon.wait_recv()
    project([(w, HALF, WIN) for w in (0, 1, 2)], 96)
    attend(0)
    li_lat.wait_recv()
    li_both.wait_recv()
    project([(3, 0, WIN)], 128)
    attend(3)
    finish([(3, 0, WIN), (0, HALF, WIN)])
    for copy in to_lat:
        copy.start()
    to_lon(3).start()
    to_lon(0).start()
    attend(1)
    attend(2)
    finish([(1, HALF, WIN), (2, HALF, WIN)])
    to_lon(1).start()
    to_lon(2).start()
    finish([(w, 0, HALF) for w in (0, 1, 2)])
    OA[0] = dot(PA[0, :, 0 : 2 * WIN], Z[1:3].reshape(2 * WIN, D1)).astype(BF)
    for b in (1, 2):
        OA[b] = dot(PA[b], Z[b : b + 3].reshape(3 * WIN, D1)).astype(BF)
    for copy in to_lat:
        copy.wait_recv()
    for w in (3, 0, 1, 2):
        to_lon(w).wait_recv()
    for b in range(3):
        back = dot(PB[b], ZB[b : b + 3].reshape(3 * HALF, D1))
        if b == 0:
            back = back + dot(PC[...], Z[0])
        out[:, 8 * b : 8 * b + 8, :] = (OA[b].astype(F32) + back).astype(BF).reshape(24, 8, D1)

    for copy in [*own, *wx, ws, w4x, w4s, w4r, *wr, sk_lat, *sk_lon, sk_both, *li, *to_lat]:
        copy.wait_send()

    @pl.when(jnp.logical_not(is_home))
    def _():
        own_sib.wait_send()

    for s in (1, 2, 3):
        for way, k, here, onward in ring_steps(s):
            if onward:

                @pl.when(here)
                def _(way=way, k=k):
                    relay(k, way, pl.ds(0, 144), 0).wait_send()

    for k in range(8):

        @pl.when(base + 8 * c + k != lon)
        def _(k=k):
            term(k).wait_send()

    for w in range(4):
        to_lon(w).wait_send()


def local(
    skip,
    coarse,
    offsets,
    bands,
    qkv3_weight,
    out3_weight,
    up_weight,
    qkv1_weight,
    out1_weight,
    mlp_in,
    mlp_out,
):
    cells = jnp.transpose(coarse, (1, 2, 0, 3)).reshape(CELLS3 // 2, 2, D3)
    vmem = pl.BlockSpec(memory_space=pltpu.VMEM)
    smem = pl.BlockSpec(memory_space=pltpu.SMEM)
    hbm = pl.BlockSpec(memory_space=ANY)
    dma = pltpu.SemaphoreType.DMA
    placed = pl.pallas_call(
        kernel,
        out_shape=jax.ShapeDtypeStruct((24, 24, D1), BF),
        in_specs=[smem, smem, vmem] + [hbm] * 8,
        out_specs=vmem,
        scratch_shapes=[
            pltpu.VMEM((144, 512), BF),
            pltpu.VMEM((8, 144, 512), BF),
            pltpu.VMEM((3, 4, HEAD, D3), BF),
            pltpu.VMEM((64, D3), BF),
            pltpu.VMEM((D3, D1), BF),
            pltpu.VMEM((256, D1), BF),
            pltpu.VMEM((48, D1), F32),
            pltpu.VMEM((128, D1), BF),
            pltpu.VMEM((1056, D1), BF),
            pltpu.VMEM((4, WIN, D1), BF),
            pltpu.VMEM((4, WIN, WIN), F32),
            pltpu.VMEM((4, WIN, 128), BF),
            pltpu.VMEM((3, 192, 3 * WIN), BF),
            pltpu.VMEM((3, 192, 3 * HALF), BF),
            pltpu.VMEM((192, WIN), BF),
            pltpu.VMEM((3, 192, D1), BF),
            pltpu.VMEM((144, D3), BF),
            pltpu.VMEM((144, 768), BF),
            pltpu.VMEM((8, 144, 128), BF),
            pltpu.VMEM((8, 144, 128), BF),
            pltpu.VMEM((128, D1), BF),
            pltpu.VMEM((D1, 3 * D1), BF),
            pltpu.VMEM((D1, 3 * D1), BF),
            pltpu.VMEM((D1, D1), BF),
            pltpu.VMEM((D1, FF), BF),
            pltpu.VMEM((FF, D1), BF),
            pltpu.VMEM((4, WIN, 3 * D1), BF),
            pltpu.VMEM((WIN, D1), BF),
            pltpu.VMEM((4, WIN, D1), F32),
            pltpu.VMEM((5, WIN, D1), BF),
            pltpu.VMEM((5, HALF, D1), BF),
            dma((8,)),
            dma((2 * PIECES + 1,)),
            dma((8, 2)),
            dma((8, PIECES)),
            dma((4,)),
            dma((4,)),
            dma((1,)),
            dma((1,)),
            dma((4,)),
            dma((4,)),
            dma((3,)),
            dma((3,)),
            dma((4,)),
            dma((4,)),
            dma((8,)),
            dma((8,)),
            dma((3,)),
            dma((3,)),
            dma((4,)),
            dma((4,)),
            dma((3,)),
            dma((3,)),
        ],
        compiler_params=pltpu.CompilerParams(
            collective_id=0, has_side_effects=True, vmem_limit_bytes=56 * 1024 * 1024
        ),
    )(
        offsets,
        bands,
        cells,
        jnp.transpose(skip, (0, 2, 1, 3)).reshape(OWN, D1),
        qkv3_weight.T.reshape(3, HEAD, D3),
        out3_weight,
        up_weight,
        qkv1_weight,
        out1_weight,
        mlp_in,
        mlp_out,
    )
    return jnp.transpose(placed.reshape(2, 12, 24, D1), (0, 2, 1, 3))


def solution(mesh):
    return jax.shard_map(
        local,
        mesh=mesh,
        in_specs=(
            P(None, "lat", "lon", None),
            P(None, "lat", "lon", None),
            P(),
            P(),
            P(None, "lon"),
            P("lon", None),
            P(),
            P(),
            P(),
            P(),
            P(),
        ),
        out_specs=P(None, "lat", "lon", None),
        check_vma=False,
    )
```

```python
import jax
import jax.numpy as jnp
from jax import lax
from jax.experimental import pallas as pl
from jax.experimental.pallas import tpu as pltpu
from jax.sharding import PartitionSpec as P

LATS = 8
LONS = 32
ROWS = 192
D3 = 2048
D1 = 512
FF = 2048
HEAD = 64
CELLS3 = 36
OWN = 576
PIECES = 3
PIECE = 144 // PIECES
SCALE = HEAD**-0.5
EPS = 1e-05
HALF = 80
WIN = 2 * HALF
MASKED = -1e30

F32 = jnp.float32
BF = jnp.bfloat16
MESH = pl.DeviceIdType.MESH
ANY = pl.ANY


def dot(a, b):
    return jnp.dot(a, b, preferred_element_type=F32)


def dot_nt(a, b):
    return lax.dot_general(a, b, (((1,), (1,)), ((), ())), preferred_element_type=F32)


def normalize(values):
    centred = values - jnp.mean(values, axis=-1, keepdims=True)
    spread = jnp.mean(centred * centred, axis=-1, keepdims=True)
    return centred * lax.rsqrt(spread + EPS)


def column(n):
    return lax.broadcasted_iota(jnp.int32, (n, 1), 0)


def onehot(target, width):
    n = target.shape[0]
    hit = lax.broadcasted_iota(jnp.int32, (n, width), 1) == target
    return jnp.where(hit, 1.0, 0.0).astype(BF)


def frame_cell(n):
    half = (n >= HALF).astype(jnp.int32)
    m = n - HALF * half
    valid = m < 72
    sixth = (m * 43) >> 8
    return valid, sixth & 1, 5 - (sixth >> 1), m - 6 * sixth + 6 * half


def pair_mix(q, k, v, allowed):
    low = lax.broadcasted_iota(jnp.int32, q.shape, 1) < HEAD
    sums = []
    for here in (low, jnp.logical_not(low)):
        scores = dot_nt(jnp.where(here, q, jnp.zeros_like(q)), k)
        if allowed is not None:
            scores = scores + allowed
        weights = jnp.exp(scores - jnp.max(scores, axis=1, keepdims=True)).astype(BF)
        sums.append(dot(weights, jnp.where(here, v, jnp.ones_like(v))))
    total = pltpu.roll(jnp.where(low, sums[1], sums[0]), HEAD, 1)
    return jnp.where(low, sums[0], sums[1]) * (1.0 / total)


def kernel(
    offs,
    bands,
    coarse,
    skip,
    wq,
    wo,
    up,
    w1,
    wo1,
    wi,
    wf,
    out,
    xs,
    G,
    Wb,
    wov,
    upv,
    W4,
    cup,
    Sp,
    E,
    skF,
    bias,
    Pl,
    PA,
    PB,
    PC,
    OA,
    Xt,
    PK,
    msg,
    R,
    LE,
    w1v,
    w1p,
    wo1v,
    wiv,
    wfv,
    pk1,
    mix,
    AT,
    Z,
    ZB,
    loc,
    own_send,
    ring_send,
    ring_recv,
    wx_send,
    wx_recv,
    ws_send,
    ws_recv,
    wr_send,
    wr_recv,
    w4_send,
    w4_recv,
    sk_send,
    sk_recv,
    aa_send,
    aa_recv,
    li_send,
    li_recv,
    lo_send,
    lo_recv,
    la_send,
    la_recv,
):
    lat = lax.axis_index("lat")
    lon = lax.axis_index("lon")
    xl = lon // 16
    z = lax.rem(lon // 2, 8)
    c = lax.rem(lon, 2)
    base = xl * 16

    def at(lat_, lon_):
        return {"lat": lat_, "lon": lon_}

    def chip(z_, c_):
        return at(lat, base + 2 * lax.rem(z_ + 8, 8) + c_)

    sibling = at(lat, lon + 1 - 2 * c)
    across = lax.rem(lon + 16, 32)
    near = at(lat, across)
    far = at(lat + 1 - 2 * lax.rem(lat, 2), across)
    lon_next = lax.rem(lon + 1, LONS)
    lon_prev = lax.rem(lon + LONS - 1, LONS)
    lat_next = lax.rem(lat + 1, LATS)
    lat_prev = lax.rem(lat + LATS - 1, LATS)

    def remote(src, dst, send, recv, device):
        return pltpu.make_async_remote_copy(
            src_ref=src, dst_ref=dst, send_sem=send, recv_sem=recv, device_id=device, device_id_type=MESH
        )

    loads = [
        pltpu.make_async_copy(src, dst, loc.at[i])
        for i, (src, dst) in enumerate(
            [(up, upv), (wo, wov), (wq, Wb.at[:, 0]), (skip, E.at[0:OWN]), (w1, w1v), (wo1, wo1v), (wi, wiv), (wf, wfv)]
        )
    ]
    for load in loads:
        load.start()

    barrier = pltpu.get_barrier_semaphore()
    greeted = [chip(z + d, c_) for d in range(1, 8) for c_ in (0, 1)] + [
        sibling,
        near,
        far,
        at(lat, lon_next),
        at(lat, lon_prev),
        at(lat_next, lon),
        at(lat_prev, lon),
        at(lat_next, lon_next),
        at(lat_prev, lon_prev),
    ]
    for device in greeted:
        pl.semaphore_signal(barrier, inc=1, device_id=device, device_id_type=MESH)

    cells = coarse[...].astype(F32).reshape(CELLS3, D3)
    cells = jnp.concatenate([cells, jnp.zeros((12, D3), F32)], axis=0)
    normed3 = normalize(cells).astype(BF)
    cells = cells.astype(BF)
    rest = jnp.zeros((16, 512), F32)
    i16 = column(16)
    for f in range(4):
        part = normed3[:, 512 * f : 512 * f + 512]
        xs[32 * f : 32 * f + 32, :] = part[0:32]
        pick = onehot(jnp.where((i16 >> 2) == f, i16 & 3, -1), 16)
        rest = rest + dot(pick, part[32:48])
    xs[128:144, :] = rest.astype(BF)

    for first in (64, 144):
        Z[0, first : first + 16, :] = jnp.zeros((16, D1), BF)
    ZB[0, 64:80, :] = jnp.zeros((16, D1), BF)

    pl.semaphore_wait(barrier, len(greeted))

    target = z // 4
    mine = lax.rem(z, 4) * 2 + c
    is_home = target == c

    def piece(t):
        return pl.ds(PIECE * t, PIECE)

    own = [
        remote(
            xs.at[piece(t)],
            G.at[mine, piece(t)],
            own_send.at[2 * t + way],
            ring_recv.at[mine, t],
            chip(z + 1 - 2 * way, target),
        )
        for t in range(PIECES)
        for way in (0, 1)
    ]
    own_sib = remote(xs, G.at[mine], own_send.at[2 * PIECES], ring_recv.at[mine, 0], sibling)
    for copy in own:
        copy.start()

    @pl.when(jnp.logical_not(is_home))
    def _():
        own_sib.start()

    def rows(j):
        return pl.ds(16 * j, 16)

    wx = [
        remote(wq.at[:, rows(j)], Wb.at[:, 2, rows(j)], wx_send.at[j], wx_recv.at[j], near if j < 2 else far)
        for j in (0, 2, 1, 3)
    ]
    for copy in wx:
        copy.start()
    ws = remote(wq, Wb.at[:, 1], ws_send.at[0], ws_recv.at[0], sibling)
    ws.start()

    loads[0].wait()
    loads[1].wait()
    W4[0:64, :] = dot(wov[...], upv[...]).astype(BF)
    w4x = remote(W4.at[0:64], W4.at[128:192], w4_send.at[0], w4_recv.at[0], near)
    w4x.start()
    w4s = remote(W4.at[0:64], W4.at[64:128], w4_send.at[1], w4_recv.at[1], sibling)
    w4s.start()
    cup[...] = dot(cells, upv[...])

    @pl.when(is_home)
    def _():
        G[pl.ds(mine, 1)] = xs[...].reshape(1, 144, 512)

    def relay(k, way, rows_, t):
        block = G.at[k, rows_]
        return remote(block, block, ring_send.at[k, way], ring_recv.at[k, t], chip(z + 1 - 2 * way, c))

    def ring_steps(s):
        for way in (0, 1):
            source = lax.rem(z + (8 - s if way == 0 else s), 8)
            for core in (0, 1):
                limit = 4 if core == way else 3
                if s <= limit:
                    yield way, lax.rem(source, 4) * 2 + core, source // 4 == c, s < limit

    def ring(s):
        for t in range(PIECES):
            for way, k, here, onward in ring_steps(s):

                @pl.when(here)
                def _(way=way, k=k, onward=onward, t=t):
                    copy = relay(k, way, piece(t), t)
                    copy.wait_recv()
                    if onward:
                        copy.start()

    loads[3].wait()
    r128 = column(128)
    r64 = r128 & 63
    ten = (r64 * 103) >> 10
    five = (r64 * 205) >> 10
    first_rows = (five & 1) * 288 + (ten + 6 * (r128 >> 6)) * 24 + r64 - 5 * five
    Sp[...] = dot(onehot(jnp.where(r64 < 60, first_rows, -1), OWN), E[0:OWN, :]).astype(BF)

    sk_lat = remote(Sp, E.at[864:992], sk_send.at[2], sk_recv.at[2], at(lat_prev, lon))
    sk_lat.start()

    ring(1)

    ring(2)

    ring(3)

    sk_lon = [
        remote(E.at[0:144], E.at[576:720], sk_send.at[0], sk_recv.at[0], at(lat, lon_prev)),
        remote(E.at[288:432], E.at[720:864], sk_send.at[1], sk_recv.at[1], at(lat, lon_prev)),
    ]
    for copy in sk_lon:
        copy.start()

    loads[4].wait()
    for pair in range(4):
        for part in range(3):
            first = 384 * pair + 64 * part
            both = jnp.concatenate([w1v[:, first : first + 64], w1v[:, first + 192 : first + 256]], axis=1)
            if part == 0:
                both = (both.astype(F32) * SCALE).astype(BF)
            w1p[:, 512 * part + 128 * pair : 512 * part + 128 * pair + 128] = both

    w4x.wait_recv()
    w4r = remote(W4.at[128:192], W4.at[192:256], w4_send.at[2], w4_recv.at[2], sibling)
    w4r.start()
    wr = [
        remote(Wb.at[:, 2, rows(j)], Wb.at[:, 3, rows(j)], wr_send.at[j], wr_recv.at[j], sibling) for j in (0, 2, 1, 3)
    ]
    for arrived, onward in zip(wx, wr):
        arrived.wait_recv()
        onward.start()

    sk_lat.wait_recv()
    sk_both = remote(E.at[864:928], E.at[992:1056], sk_send.at[3], sk_recv.at[3], at(lat, lon_prev))
    sk_both.start()

    @pl.when(is_home)
    def _():
        k = lax.rem(z, 4) * 2 + (1 - c)
        remote(xs, G.at[k], own_send.at[0], ring_recv.at[k, 0], sibling).wait_recv()

    loads[2].wait()
    ws.wait_recv()
    for copy in wr:
        copy.wait_recv()
    w4s.wait_recv()
    w4r.wait_recv()

    def term(k):
        return remote(msg.at[k], R.at[z], aa_send.at[k], aa_recv.at[z], at(lat, base + 8 * c + k))

    i64 = column(64)

    def level3(w):
        tails = G[pl.ds(4 * w, 4), 128:144, :].reshape(64, 512)
        for f in range(4):
            lanes = slice(512 * f, 512 * f + 512)
            Xt[0:128, lanes] = G[pl.ds(4 * w, 4), 32 * f : 32 * f + 32, :].reshape(128, 512)
            Xt[128:144, lanes] = dot(onehot((i16 >> 2) * 16 + 4 * f + (i16 & 3), 64), tails).astype(BF)
        packed = dot_nt(Xt[...], Wb[...].reshape(768, D3))
        PK[:, 0:256] = (packed[:, 0:256] * SCALE).astype(BF)
        PK[:, 256:768] = packed[:, 256:768].astype(BF)
        terms = jnp.zeros((144, 512), F32)
        for pair in range(2):
            q, k, v = (PK[:, 256 * i + 128 * pair : 256 * i + 128 * pair + 128] for i in range(3))
            terms = terms + dot(pair_mix(q, k, v, None).astype(BF), W4[128 * pair : 128 * pair + 128, :])
        terms = terms.astype(BF)
        tails = jnp.zeros((64, 128), F32)
        for f in range(4):
            part = terms[:, 128 * f : 128 * f + 128]
            msg[pl.ds(4 * w, 4), 32 * f : 32 * f + 32, :] = part[0:128].reshape(4, 32, 128)
            tails = tails + dot(
                onehot(jnp.where(((i64 >> 2) & 3) == f, (i64 >> 4) * 4 + (i64 & 3), -1), 16), part[128:144]
            )
        msg[pl.ds(4 * w, 4), 128:144, :] = tails.astype(BF).reshape(4, 16, 128)
        for q in range(4):
            k = 4 * w + q

            @pl.when(base + 8 * c + k != lon)
            def _(k=k):
                term(k).start()

    flank = lax.rem(z, 4) // 2
    away = lax.rem(target + c, 2)
    nearer = flank + away * (1 - 2 * flank)
    level3(nearer)
    ring(4)
    level3(1 - nearer)

    @pl.when(is_home)
    def _():
        R[pl.ds(z, 1)] = msg[pl.ds(mine, 1)]

    a = offs[0]
    shift_lat = jnp.where(a >= 6, a - 6, a)
    shift_lon = offs[1]
    n = column(WIN)
    valid, level, row, col = frame_cell(n)
    valid_t, _, row_t, _ = frame_cell(lax.broadcasted_iota(jnp.int32, (1, WIN), 1))
    source_col = col + shift_lon
    for w in range(4):
        source_row = row + (shift_lat + 6 * w)
        coarse_row = source_row >> 2
        coarse_col = source_col >> 2
        row_out = (coarse_row >= 6).astype(jnp.int32)
        col_out = (coarse_col >= 3).astype(jnp.int32)
        cell = 48 * col_out + row_out * (96 - 32 * col_out) + level + 6 * (coarse_row - 6 * row_out) + 2 * (coarse_col - 3 * col_out)
        Pl[w] = onehot(jnp.where(valid, cell, -1), 128)
        label = jnp.zeros((WIN, 1), jnp.int32)
        label_t = jnp.zeros((1, WIN), jnp.int32)
        for i in range(6):
            band = bands[lax.rem(lat * 24 + shift_lat + (6 * w + i), ROWS)]
            label = jnp.where(row == i, band, label)
            label_t = jnp.where(row_t == i, band, label_t)
        free = jnp.where(valid, 0, 1)
        seen = jnp.where(valid_t, 1, 0)
        match = jnp.where(label == label_t, 1, 0)
        bias[w] = jnp.where(seen * (match + free) > 0, 0.0, MASKED)

    for copy in sk_lon:
        copy.wait_recv()
    sk_both.wait_recv()
    for w in range(4):
        source_row = row + (shift_lat + 6 * w)
        cell = jnp.where(
            source_col < 12,
            288 * level + 24 * source_col + source_row,
            576 + 144 * level + 24 * (source_col - 12) + source_row,
        )
        third = (source_col >= 6).astype(jnp.int32) + (source_col >= 12).astype(jnp.int32)
        below = 864 + 64 * third + 10 * (source_col - 6 * third) + 5 * level + source_row - 24
        cell = jnp.where(source_row < 24, cell, below)
        width = 1056 if w == 3 else 864
        skF[w] = dot(onehot(jnp.where(valid, cell, -1), width), E[0:width, :]).astype(BF)

    total = jnp.zeros((144, 128), F32)
    for s in range(8):

        @pl.when(base + 2 * s + target != lon)
        def _(s=s):
            remote(msg.at[0], R.at[s], aa_send.at[0], aa_recv.at[s], sibling).wait_recv()

    for s in range(8):
        total = total + R[s].astype(F32)
    for f in range(4):
        lanes = slice(128 * f, 128 * f + 128)
        LE[0:32, lanes] = (cup[0:32, lanes] + total[32 * f : 32 * f + 32]).astype(BF)
        rest = jnp.concatenate([total[128 + 4 * f : 132 + 4 * f], jnp.zeros((12, 128), F32)], axis=0)
        LE[32:48, lanes] = (cup[32:48, lanes] + rest).astype(BF)

    li_lon = remote(LE.at[0:48], LE.at[48:96], li_send.at[0], li_recv.at[0], at(lat, lon_prev))
    li_lat = remote(LE.at[0:16], LE.at[96:112], li_send.at[1], li_recv.at[1], at(lat_prev, lon))
    li_both = remote(LE.at[0:16], LE.at[112:128], li_send.at[2], li_recv.at[2], at(lat_prev, lon_prev))
    li = [li_both, li_lat, li_lon]
    for copy in li:
        copy.start()

    for load in loads[5:]:
        load.wait()

    def project(parts, reach):
        chosen = jnp.concatenate([Pl[w, first:last, 0:reach] for w, first, last in parts], axis=0)
        taken = jnp.concatenate([skF[w, first:last, :] for w, first, last in parts], axis=0)
        stream = taken.astype(F32) + dot(chosen, LE[0:reach, :])
        packed = dot(normalize(stream).astype(BF), w1p[...]).astype(BF)
        at_row = 0
        for w, first, last in parts:
            here = slice(at_row, at_row + last - first)
            AT[w, first:last, :] = stream[here]
            pk1[w, first:last, :] = packed[here]
            at_row += last - first

    def attend(w):
        for pair in range(4):
            lanes = slice(128 * pair, 128 * pair + 128)
            q, k, v = (pk1[w, :, 512 * i + 128 * pair : 512 * i + 128 * pair + 128] for i in range(3))
            mix[:, lanes] = pair_mix(q, k, v, bias[w]).astype(BF)
        AT[w] = AT[w] + dot(mix[...], wo1v[...])

    def finish(parts):
        attended = jnp.concatenate([AT[w, first:last, :] for w, first, last in parts], axis=0)
        normed2 = normalize(attended).astype(BF)
        result = attended
        for f in range(2):
            hidden = jax.nn.gelu(dot(normed2, wiv[:, 1024 * f : 1024 * f + 1024])).astype(BF)
            result = result + dot(hidden, wfv[1024 * f : 1024 * f + 1024, :])
        result = result.astype(BF)
        at_row = 0
        for w, first, last in parts:
            Z[w + 1, first:last, :] = result[at_row : at_row + last - first]
            at_row += last - first

    def to_lon(w):
        return remote(
            Z.at[w + 1, HALF:WIN], ZB.at[w + 1], lo_send.at[w], lo_recv.at[w], at(lat, lon_next)
        )

    to_lat = [
        remote(Z.at[4, 80:144], ZB.at[0, 0:64], la_send.at[2], la_recv.at[2], at(lat_next, lon_next)),
        remote(Z.at[4, 80:144], Z.at[0, 80:144], la_send.at[1], la_recv.at[1], at(lat_next, lon)),
        remote(Z.at[4, 0:64], Z.at[0, 0:64], la_send.at[0], la_recv.at[0], at(lat_next, lon)),
    ]
    project([(w, 0, HALF) for w in (0, 1, 2)], 48)
    li_lon.wait_recv()
    project([(w, HALF, WIN) for w in (0, 1, 2)], 96)
    li_lat.wait_recv()
    li_both.wait_recv()
    project([(3, 0, WIN)], 128)
    attend(3)
    finish([(3, 0, WIN)])
    for copy in to_lat:
        copy.start()
    to_lon(3).start()
    attend(0)
    attend(1)
    finish([(0, HALF, WIN), (1, HALF, WIN)])
    to_lon(0).start()
    to_lon(1).start()
    attend(2)
    finish([(2, HALF, WIN)])
    to_lon(2).start()
    finish([(w, 0, HALF) for w in (0, 1, 2)])

    r = column(192)
    out_level = (r >= 96).astype(jnp.int32)
    frame_col = ((r - 96 * out_level) >> 3) - shift_lon
    left = frame_col < 0
    second = (frame_col >= 6).astype(jnp.int32)
    for b in range(3):
        frame_row = (r & 7) + (8 * b + 6) - shift_lat
        slot = (frame_row * 43) >> 8
        inner = 12 * (5 - (frame_row - 6 * slot)) + 6 * out_level + frame_col
        kept = WIN * (slot - max(b, 1)) + (HALF - 6) * second + inner
        PA[b] = onehot(jnp.where(left, -1, kept), 3 * WIN)
        PB[b] = onehot(jnp.where(left, HALF * (slot - b) + inner + 6, -1), 3 * HALF)
        if b == 0:
            PC[...] = onehot(jnp.where(left | (slot > 0), -1, kept + WIN), WIN)

    OA[0] = dot(PA[0, :, 0 : 2 * WIN], Z[1:3].reshape(2 * WIN, D1)).astype(BF)
    for b in (1, 2):
        OA[b] = dot(PA[b], Z[b : b + 3].reshape(3 * WIN, D1)).astype(BF)
    for copy in to_lat:
        copy.wait_recv()
    for w in (3, 0, 1, 2):
        to_lon(w).wait_recv()
    for b in range(3):
        back = dot(PB[b], ZB[b : b + 3].reshape(3 * HALF, D1))
        if b == 0:
            back = back + dot(PC[...], Z[0])
        out[:, 8 * b : 8 * b + 8, :] = (OA[b].astype(F32) + back).astype(BF).reshape(24, 8, D1)

    for copy in [*own, *wx, ws, w4x, w4s, w4r, *wr, sk_lat, *sk_lon, sk_both, *li, *to_lat]:
        copy.wait_send()

    @pl.when(jnp.logical_not(is_home))
    def _():
        own_sib.wait_send()

    for s in (1, 2, 3):
        for way, k, here, onward in ring_steps(s):
            if onward:

                @pl.when(here)
                def _(way=way, k=k):
                    relay(k, way, pl.ds(0, 144), 0).wait_send()

    for k in range(8):

        @pl.when(base + 8 * c + k != lon)
        def _(k=k):
            term(k).wait_send()

    for w in range(4):
        to_lon(w).wait_send()


def local(
    skip,
    coarse,
    offsets,
    bands,
    qkv3_weight,
    out3_weight,
    up_weight,
    qkv1_weight,
    out1_weight,
    mlp_in,
    mlp_out,
):
    cells = jnp.transpose(coarse, (1, 2, 0, 3)).reshape(CELLS3 // 2, 2, D3)
    vmem = pl.BlockSpec(memory_space=pltpu.VMEM)
    smem = pl.BlockSpec(memory_space=pltpu.SMEM)
    hbm = pl.BlockSpec(memory_space=ANY)
    dma = pltpu.SemaphoreType.DMA
    placed = pl.pallas_call(
        kernel,
        out_shape=jax.ShapeDtypeStruct((24, 24, D1), BF),
        in_specs=[smem, smem, vmem] + [hbm] * 8,
        out_specs=vmem,
        scratch_shapes=[
            pltpu.VMEM((144, 512), BF),
            pltpu.VMEM((8, 144, 512), BF),
            pltpu.VMEM((3, 4, HEAD, D3), BF),
            pltpu.VMEM((64, D3), BF),
            pltpu.VMEM((D3, D1), BF),
            pltpu.VMEM((256, D1), BF),
            pltpu.VMEM((48, D1), F32),
            pltpu.VMEM((128, D1), BF),
            pltpu.VMEM((1056, D1), BF),
            pltpu.VMEM((4, WIN, D1), BF),
            pltpu.VMEM((4, WIN, WIN), F32),
            pltpu.VMEM((4, WIN, 128), BF),
            pltpu.VMEM((3, 192, 3 * WIN), BF),
            pltpu.VMEM((3, 192, 3 * HALF), BF),
            pltpu.VMEM((192, WIN), BF),
            pltpu.VMEM((3, 192, D1), BF),
            pltpu.VMEM((144, D3), BF),
            pltpu.VMEM((144, 768), BF),
            pltpu.VMEM((8, 144, 128), BF),
            pltpu.VMEM((8, 144, 128), BF),
            pltpu.VMEM((128, D1), BF),
            pltpu.VMEM((D1, 3 * D1), BF),
            pltpu.VMEM((D1, 3 * D1), BF),
            pltpu.VMEM((D1, D1), BF),
            pltpu.VMEM((D1, FF), BF),
            pltpu.VMEM((FF, D1), BF),
            pltpu.VMEM((4, WIN, 3 * D1), BF),
            pltpu.VMEM((WIN, D1), BF),
            pltpu.VMEM((4, WIN, D1), F32),
            pltpu.VMEM((5, WIN, D1), BF),
            pltpu.VMEM((5, HALF, D1), BF),
            dma((8,)),
            dma((2 * PIECES + 1,)),
            dma((8, 2)),
            dma((8, PIECES)),
            dma((4,)),
            dma((4,)),
            dma((1,)),
            dma((1,)),
            dma((4,)),
            dma((4,)),
            dma((3,)),
            dma((3,)),
            dma((4,)),
            dma((4,)),
            dma((8,)),
            dma((8,)),
            dma((3,)),
            dma((3,)),
            dma((4,)),
            dma((4,)),
            dma((3,)),
            dma((3,)),
        ],
        compiler_params=pltpu.CompilerParams(
            collective_id=0, has_side_effects=True, vmem_limit_bytes=56 * 1024 * 1024
        ),
    )(
        offsets,
        bands,
        cells,
        jnp.transpose(skip, (0, 2, 1, 3)).reshape(OWN, D1),
        qkv3_weight.T.reshape(3, HEAD, D3),
        out3_weight,
        up_weight,
        qkv1_weight,
        out1_weight,
        mlp_in,
        mlp_out,
    )
    return jnp.transpose(placed.reshape(2, 12, 24, D1), (0, 2, 1, 3))


def solution(mesh):
    return jax.shard_map(
        local,
        mesh=mesh,
        in_specs=(
            P(None, "lat", "lon", None),
            P(None, "lat", "lon", None),
            P(),
            P(),
            P(None, "lon"),
            P("lon", None),
            P(),
            P(),
            P(),
            P(),
            P(),
        ),
        out_specs=P(None, "lat", "lon", None),
        check_vma=False,
    )
```
